128 devices in a mesh: ctx: 16 (over y_hi, z, core), chan: 8 (over x, y_lo).
Axes of the slice: x: 4, y: 4 (y_hi: 2, y_lo: 2; y = y_hi * 2 + y_lo), z: 4, core: 2. Of those that a mesh axis runs over, the one named last changes fastest.
Arguments:
- tokens: bfloat16 [1, 262144, 768], P(None, ('ctx', 'chan')), may hold values from -6 to 6
- norm_gain: float32 [768], replicated, may hold values from 0.1 to 1.9
- block_weights: bfloat16 [512, 512, 512], P(('ctx', 'chan')), may hold values from -0.25 to 0.25
- stride_weights: bfloat16 [512, 512, 512], P(('ctx', 'chan')), may hold values from -0.25 to 0.25
- proj_weights: bfloat16 [3, 768, 768], P(None, 'chan'), may hold values from -11 to 11
- proj_scales: float32 [3, 768], replicated, may hold values from 0.5 to 2
Outputs:
- layer_output: bfloat16 [1, 262144, 768], P(None, ('ctx', 'chan'))
The draws below stay inside these ranges and needn't reach their ends.
All inputs are finite; a program needn't handle non-finite values.
Results may differ from the reference program's by a relative error of at most 0.017.
Values may be sent and summed in bfloat16 or wider, within the bound.
A program may use at most 128 MiB of HBM per device.

```python
import math
import jax
import jax.numpy as jnp
from jax import lax

C = 768
NB = 512
BS = 512
SEQS = 1
L = 262144


def draw_proj_weights(key, part):
    key = jax.random.fold_in(key, 7)
    key_vals, key_rows = jax.random.split(key)
    rising = jnp.arange(C, dtype=jnp.float32) / C
    spread = jax.random.uniform(key_rows, (3, C, 1), jnp.float32)
    entries = jax.random.truncated_normal(key_vals, -4.0, 4.0, (3, C, C), jnp.float32)
    scales = jnp.exp(jnp.log(3.0) * rising)[None, :, None] * jnp.exp(jnp.log(10.0) * spread)
    return (0.03 * entries * scales).astype(jnp.bfloat16)


def block_scale(stream_key, extent, cuts, smallest, high):
    factor_of = 1.0
    for position, parts in cuts:
        heights = jax.random.uniform(jax.random.fold_in(jax.random.fold_in(stream_key, 6), position), (parts,), jnp.float32, smallest / len(cuts), high / len(cuts))
        factor_of = factor_of * jnp.repeat(jnp.exp(heights), extent[position] // parts).reshape((-1,) + (1,) * (len(extent) - 1 - position))
    return factor_of


def centred(stream_key, shape, width, bound, cuts=(), kind=jnp.bfloat16):
    loudness = block_scale(stream_key, shape, cuts, -0.22, 0.18) if cuts else 1.0
    drawn = jax.random.normal(stream_key, shape, jnp.float32) * width * loudness
    return jnp.minimum(jnp.maximum(drawn, -bound), bound).astype(kind)


def setup_inputs(seed: int = 0) -> dict:
    key_list = jax.random.split(jax.random.key(seed), 7)
    tokens = centred(key_list[0], (SEQS, L, C), 1.0, 6.0, ((1, 128),))
    norm_gain = jnp.clip(1.0 + 0.18 * jax.random.normal(key_list[1], (C,), jnp.float32), 0.1, 1.9)
    block_weights = centred(key_list[2], (NB, BS, BS), BS ** -0.5, 0.25, ((0, 128),))
    stride_weights = centred(key_list[3], (BS, NB, NB), NB ** -0.5, 0.25, ((0, 128),))
    proj_weights = draw_proj_weights(jax.random.fold_in(key_list[6], 71), 0)
    proj_scales = jnp.clip(jnp.exp(jax.random.uniform(key_list[5], (3, C), jnp.float32, math.log(0.5), math.log(2.0))), 0.5, 2.0)
    return {"tokens": tokens, "norm_gain": norm_gain, "block_weights": block_weights, "stride_weights": stride_weights, "proj_weights": proj_weights, "proj_scales": proj_scales}


def reference(tokens, norm_gain, block_weights, stride_weights, proj_weights, proj_scales):
    wide_tokens = tokens.astype(jnp.float32)
    mean_square = lax.optimization_barrier(jnp.mean(wide_tokens * wide_tokens, axis=-1, keepdims=True))
    normed = (wide_tokens * lax.rsqrt(mean_square + 1e-05) * norm_gain).astype(jnp.bfloat16)
    wide_proj = proj_weights.astype(jnp.float32)
    squares = lax.optimization_barrier(jnp.sum(wide_proj * wide_proj, axis=1))
    colscale = proj_scales * lax.rsqrt(squares + 1e-06)
    flat_rows = normed.reshape(SEQS * NB * BS, C)
    value = (jnp.dot(flat_rows, proj_weights[0], preferred_element_type=jnp.float32) * colscale[0]).astype(jnp.bfloat16)
    gate = (jnp.dot(flat_rows, proj_weights[1], preferred_element_type=jnp.float32) * colscale[1]).astype(jnp.bfloat16)
    wide_block = block_weights.astype(jnp.float32)
    wide_stride = stride_weights.astype(jnp.float32)

    def mix_one(seq_value):
        grouped = seq_value.reshape(NB, BS, C).astype(jnp.float32)
        first = jnp.einsum('bts,bsc->btc', wide_block, grouped).astype(jnp.bfloat16)
        second = jnp.einsum('tab,btc->atc', wide_stride, first.astype(jnp.float32)).astype(jnp.bfloat16)
        return second.reshape(NB * BS, C)
    mixed = lax.map(mix_one, value.reshape(SEQS, NB * BS, C)).reshape(SEQS * NB * BS, C)
    wide_gate = gate.astype(jnp.float32)
    hidden = (mixed.astype(jnp.float32) * jax.nn.silu(wide_gate)).astype(jnp.bfloat16)
    result = jnp.dot(hidden, proj_weights[2], preferred_element_type=jnp.float32) * colscale[2]
    return result.astype(jnp.bfloat16).reshape(SEQS, NB * BS, C)
```

```python
import functools

import jax
import jax.numpy as jnp
from jax import lax
from jax.experimental import pallas as pl
from jax.experimental.pallas import tpu as pltpu
from jax.sharding import PartitionSpec as P

MESH = pl.DeviceIdType.MESH
ORDERS = ((0, 1, 2), (1, 2, 0), (2, 0, 1)) * 2
CHUNKS = len(ORDERS)
WIDTH = 128
PIECE = 16


def coordinates():
    c, h = lax.axis_index("ctx"), lax.axis_index("chan")
    return h // 2, (c // 8) * 2 + h % 2, (c // 2) % 4, c % 2


def device_at(x, y, z, k):
    return (y // 2) * 8 + z * 2 + k, x * 2 + y % 2


def neighbour(me, offset):
    x, y, z, k = [(m + o) % n for m, o, n in zip(me, offset, (4, 4, 4, 2))]
    return device_at(x, y, z, k)


def along(axis, step, core=0):
    offset = [0, 0, 0, core]
    offset[axis] = step
    return tuple(offset)


PARTNERS = [along(axis, step, core) for axis in range(3) for step in (1, 3, 2) for core in (0, 1)] + [(0, 0, 0, 1)]


def send_slot(order, point):
    a, b, c = order
    return point[a], point[3], point[b], point[c]


def landed_slot(order, point):
    a, b, c = order
    return point[c], point[b], point[a], point[3]


class Journey:
    def __init__(self, me, chunk, buffers, sems, first_sem):
        self.me, self.chunk, self.buffers, self.sems, self.first_sem = me, chunk, buffers, sems, first_sem

    def copies(self, hop):
        me, chunk = self.me, self.chunk
        axis = ORDERS[chunk][hop]
        source, target = self.buffers[hop], self.buffers[hop + 1]
        here = me[axis]
        send_sem, recv_sem = [s.at[self.first_sem + hop] for s in self.sems]
        local, remote = [], []
        for core in (0, 1) if hop == 0 else (0,):
            for step in (0, 1, 3, 2):
                there = (here + step) % 4
                if hop == 0:
                    src = source.at[chunk, there, (me[3] + core) % 2]
                    dst = target.at[chunk, here, me[3]]
                elif hop == 1:
                    src, dst = source.at[chunk, :, :, there], target.at[chunk, here]
                else:
                    src, dst = source.at[chunk, :, :, :, there], target.at[chunk, here]
                offset = along(axis, step, core)
                if offset == (0, 0, 0, 0):
                    local.append((src, dst, recv_sem))
                else:
                    remote.append((src, dst, send_sem, recv_sem, neighbour(me, offset)))
        return local, remote

    def start(self, hop):
        local, remote = self.copies(hop)
        for src, dst, send_sem, recv_sem, device in remote:
            pltpu.make_async_remote_copy(
                src_ref=src, dst_ref=dst, send_sem=send_sem, recv_sem=recv_sem, device_id=device, device_id_type=MESH
            ).start()
        for src, dst, sem in local:
            pltpu.make_async_copy(src, dst, sem).start()


    def wait(self, hop):
        whole = self.buffers[hop + 1].at[self.chunk]
        pltpu.make_async_copy(whole, whole, self.sems[1].at[self.first_sem + hop]).wait()

    def wait_sent(self, hop, rows):
        if hop == 0:
            sent = rows.at[:, pl.ds(0, 448), :]
        else:
            sent = self.buffers[hop].at[self.chunk, pl.ds(0, 3)]
        pltpu.make_async_copy(sent, sent, self.sems[0].at[self.first_sem + hop]).wait()


def each_octet(body):
    def step(m, carry):
        body(m, m // 8, (m // 2) % 4, m % 2)
        return carry

    lax.fori_loop(0, 16, step, 0)


def mix_kernel(
    tokens,
    gain,
    block_w,
    stride_w,
    out,
    normed,
    block_v,
    stride_v,
    wide,
    rows,
    mixed,
    fwd0,
    fwd1,
    fwd2,
    fwd3,
    ret0,
    ret1,
    ret2,
    ret3,
    out_v,
    load_sems,
    out_sems,
    send_sems,
    recv_sems,
):
    me = coordinates()
    sems = (send_sems, recv_sems)
    loads = [pltpu.make_async_copy(tokens.at[b], normed.at[b], load_sems.at[b]) for b in range(4)]
    loads.append(pltpu.make_async_copy(block_w, block_v, load_sems.at[4]))
    loads.append(pltpu.make_async_copy(stride_w, stride_v, load_sems.at[5]))
    for load in loads:
        load.start()
    barrier = pltpu.get_barrier_semaphore()
    for offset in PARTNERS:
        pl.semaphore_signal(barrier, inc=1, device_id=neighbour(me, offset), device_id_type=MESH)

    for b in range(4):
        loads[b].wait()

        def norm(i, carry, b=b):
            r = pl.ds(pl.multiple_of(i * 64, 64), 64)
            x = normed[b, r, :].astype(jnp.float32)
            scale = lax.rsqrt(jnp.mean(x * x, axis=-1, keepdims=True) + 1e-05)
            normed[b, r, :] = (x * scale * gain[...]).astype(jnp.bfloat16)
            return carry

        lax.fori_loop(0, 8, norm, 0)
    loads[4].wait()

    forward = [Journey(me, c, (fwd0, fwd1, fwd2, fwd3), sems, 3 * c) for c in range(CHUNKS)]
    back = [Journey(me, c, (ret0, ret1, ret2, ret3), sems, 3 * (CHUNKS + c)) for c in range(CHUNKS)]

    low = lax.broadcasted_iota(jnp.int32, (8, WIDTH), 0) < 4

    def paired(p, q):
        return jnp.where(low, p, pltpu.roll(q, 4, 0)), jnp.where(low, pltpu.roll(p, 4, 0), q)

    for g in range(CHUNKS // 2):
        for b in range(4):
            x = jnp.dot(block_v[b], normed[b, :, pl.ds(g * 256, 256)], preferred_element_type=jnp.float32)
            for half in range(2):
                wide[half, pl.ds(b, 512, stride=4), :] = x[:, half * WIDTH : (half + 1) * WIDTH]
        for half in range(2):
            chunk = 2 * g + half

            def pack(m, y_hi, z, core, half=half, chunk=chunk):
                for x in range(4):
                    for y_lo in range(2):
                        r = pl.ds(pl.multiple_of((m * 8 + x * 2 + y_lo) * PIECE, PIECE), PIECE)
                        slot = send_slot(ORDERS[chunk], (x, y_hi * 2 + y_lo, z, core))
                        fwd0[(chunk, *slot)] = wide[half, r, :].astype(jnp.bfloat16)

            each_octet(pack)
            if chunk == 0:
                pl.semaphore_wait(barrier, len(PARTNERS))
            forward[chunk].start(0)

    for hop in range(2):
        for chunk in range(CHUNKS):
            forward[chunk].wait(hop)
            forward[chunk].start(hop + 1)
    loads[5].wait()

    for chunk in range(CHUNKS):
        forward[chunk].wait(2)

        def split(m, y_hi, z, core, chunk=chunk):
            per_t = [[] for _ in range(4)]
            for x in range(4):
                even, odd = [
                    fwd3[(chunk, *landed_slot(ORDERS[chunk], (x, y_hi * 2 + y_lo, z, core)))].astype(jnp.float32)
                    for y_lo in range(2)
                ]
                for j in range(2):
                    first, second = paired(even[8 * j : 8 * j + 8], odd[8 * j : 8 * j + 8])
                    per_t[2 * j].append(first)
                    per_t[2 * j + 1].append(second)
            r = pl.ds(pl.multiple_of(m * 32, 32), 32)
            for t in range(4):
                rows[t, r, :] = jnp.concatenate(per_t[t], axis=0).astype(jnp.bfloat16)

        each_octet(split)
        for t in range(4):
            mixed[t] = jnp.dot(stride_v[t], rows[t], preferred_element_type=jnp.float32)

        def join(m, y_hi, z, core, chunk=chunk):
            for x in range(4):
                r = pl.ds(pl.multiple_of(m * 32 + x * 8, 8), 8)
                top = paired(mixed[0, r, :], mixed[1, r, :])
                bottom = paired(mixed[2, r, :], mixed[3, r, :])
                for y_lo in range(2):
                    slot = send_slot(ORDERS[chunk], (x, y_hi * 2 + y_lo, z, core))
                    ret0[(chunk, *slot)] = jnp.concatenate([top[y_lo], bottom[y_lo]], axis=0).astype(jnp.bfloat16)

        each_octet(join)
        back[chunk].start(0)

    for hop in range(2):
        for chunk in range(CHUNKS):
            back[chunk].wait(hop)
            back[chunk].start(hop + 1)

    stores = []
    for chunk in range(CHUNKS):
        back[chunk].wait(2)

        def unpack(m, y_hi, z, core, chunk=chunk):
            for x in range(4):
                for y_lo in range(2):
                    r = pl.ds(pl.multiple_of((m * 8 + x * 2 + y_lo) * PIECE, PIECE), PIECE)
                    slot = landed_slot(ORDERS[chunk], (x, y_hi * 2 + y_lo, z, core))
                    wide[0, r, :] = ret3[(chunk, *slot)].astype(jnp.float32)

        each_octet(unpack)
        for a in range(4):
            out_v[chunk, a] = wide[0, pl.ds(a, 512, stride=4), :].astype(jnp.bfloat16)
        stores.append(
            pltpu.make_async_copy(out_v.at[chunk], out.at[:, :, pl.ds(chunk * WIDTH, WIDTH)], out_sems.at[chunk])
        )
        stores[-1].start()
    for chunk in range(CHUNKS):
        for hop in range(3):
            forward[chunk].wait_sent(hop, rows)
            back[chunk].wait_sent(hop, rows)
    for store in stores:
        store.wait()


def mix(tokens, gain, block_w, stride_w):
    sent = (CHUNKS, 4, 2, 4, 4, PIECE, WIDTH)
    half_way = (CHUNKS, 4, 4, 2, 4, PIECE, WIDTH)
    landed = (CHUNKS, 4, 4, 4, 2, PIECE, WIDTH)
    bf16, f32 = jnp.bfloat16, jnp.float32
    hbm = pl.BlockSpec(memory_space=pl.ANY)
    return pl.pallas_call(
        mix_kernel,
        out_shape=jax.ShapeDtypeStruct((4, 512, 768), bf16),
        in_specs=[hbm, pl.BlockSpec(memory_space=pltpu.VMEM), hbm, hbm],
        out_specs=hbm,
        scratch_shapes=[
            pltpu.VMEM((4, 512, 768), bf16),
            pltpu.VMEM((4, 512, 512), bf16),
            pltpu.VMEM((4, 512, 512), bf16),
            pltpu.VMEM((2, 2048, WIDTH), f32),
            pltpu.VMEM((4, 512, WIDTH), bf16),
            pltpu.VMEM((4, 512, WIDTH), f32),
            *[pltpu.VMEM(s, bf16) for s in (sent, sent, half_way, landed)],
            *[pltpu.VMEM(s, bf16) for s in (sent, sent, half_way, landed)],
            pltpu.VMEM((CHUNKS, 4, 512, WIDTH), bf16),
            pltpu.SemaphoreType.DMA((6,)),
            pltpu.SemaphoreType.DMA((CHUNKS,)),
            *[pltpu.SemaphoreType.DMA((6 * CHUNKS,)) for _ in range(2)],
        ],
        compiler_params=pltpu.CompilerParams(collective_id=0, has_side_effects=True, vmem_limit_bytes=56 << 20),
        cost_estimate=pl.CostEstimate(flops=3 << 30, bytes_accessed=40 << 20, transcendentals=0),
        name="monarch_mix",
    )(tokens, gain, block_w, stride_w)


def local(tokens, norm_gain, block_weights, stride_weights, proj_weights, proj_scales):
    channels = tokens.shape[-1]
    weights = lax.all_gather(proj_weights, "chan", axis=1, tiled=True)
    carried = mix(tokens.reshape(4, 512, channels), norm_gain.reshape(1, channels), block_weights, stride_weights)
    carried = carried.reshape(2048, channels)
    wide_weights = weights.astype(jnp.float32)
    colscale = proj_scales * lax.rsqrt(jnp.sum(wide_weights * wide_weights, axis=1) + 1e-06)
    wide_tokens = tokens.reshape(2048, channels).astype(jnp.float32)
    mean_square = jnp.mean(wide_tokens * wide_tokens, axis=-1, keepdims=True)
    normed = (wide_tokens * lax.rsqrt(mean_square + 1e-05) * norm_gain).astype(jnp.bfloat16)

    def project(rows, k):
        return (jnp.dot(rows, weights[k], preferred_element_type=jnp.float32) * colscale[k]).astype(jnp.bfloat16)

    gate = project(normed, 1).astype(jnp.float32)
    mixed = project(carried, 0).astype(jnp.float32)
    hidden = (mixed * jax.nn.silu(gate)).astype(jnp.bfloat16)
    return project(hidden, 2).reshape(tokens.shape)


def solution(mesh):
    placed = (
        P(None, ("ctx", "chan"), None),
        P(),
        P(("ctx", "chan"), None, None),
        P(("ctx", "chan"), None, None),
        P(None, "chan", None),
        P(),
    )
    return jax.shard_map(
        local, mesh=mesh, in_specs=placed, out_specs=P(None, ("ctx", "chan"), None), check_vma=False
    )
```

```python
import functools

import jax
import jax.numpy as jnp
from jax import lax
from jax.experimental import pallas as pl
from jax.experimental.pallas import tpu as pltpu
from jax.sharding import PartitionSpec as P

MESH = pl.DeviceIdType.MESH
ORDERS = ((0, 1, 2), (1, 2, 0), (2, 0, 1)) * 2
CHUNKS = len(ORDERS)
WIDTH = 128
PIECE = 16


def coordinates():
    c, h = lax.axis_index("ctx"), lax.axis_index("chan")
    return h // 2, (c // 8) * 2 + h % 2, (c // 2) % 4, c % 2


def device_at(x, y, z, k):
    return (y // 2) * 8 + z * 2 + k, x * 2 + y % 2


def neighbour(me, offset):
    x, y, z, k = [(m + o) % n for m, o, n in zip(me, offset, (4, 4, 4, 2))]
    return device_at(x, y, z, k)


def along(axis, step, core=0):
    offset = [0, 0, 0, core]
    offset[axis] = step
    return tuple(offset)


PARTNERS = [along(axis, step, core) for axis in range(3) for step in (1, 3, 2) for core in (0, 1)] + [(0, 0, 0, 1)]


def send_slot(order, point):
    a, b, c = order
    return point[a], point[3], point[b], point[c]


def landed_slot(order, point):
    a, b, c = order
    return point[c], point[b], point[a], point[3]


class Journey:
    def __init__(self, me, chunk, buffers, sems, first_sem):
        self.me, self.chunk, self.buffers, self.sems, self.first_sem = me, chunk, buffers, sems, first_sem

    def copies(self, hop):
        me, chunk = self.me, self.chunk
        axis = ORDERS[chunk][hop]
        source, target = self.buffers[hop], self.buffers[hop + 1]
        here = me[axis]
        send_sem, recv_sem = [s.at[self.first_sem + hop] for s in self.sems]
        local, remote = [], []
        for core in (0, 1) if hop == 0 else (0,):
            for step in (0, 1, 3, 2):
                there = (here + step) % 4
                if hop == 0:
                    src = source.at[chunk, there, (me[3] + core) % 2]
                    dst = target.at[chunk, here, me[3]]
                elif hop == 1:
                    src, dst = source.at[chunk, :, :, there], target.at[chunk, here]
                else:
                    src, dst = source.at[chunk, :, :, :, there], target.at[chunk, here]
                offset = along(axis, step, core)
                if offset == (0, 0, 0, 0):
                    local.append((src, dst, recv_sem))
                else:
                    remote.append((src, dst, send_sem, recv_sem, neighbour(me, offset)))
        return local, remote

    def start(self, hop):
        local, remote = self.copies(hop)
        for src, dst, send_sem, recv_sem, device in remote:
            pltpu.make_async_remote_copy(
                src_ref=src, dst_ref=dst, send_sem=send_sem, recv_sem=recv_sem, device_id=device, device_id_type=MESH
            ).start()
        for src, dst, sem in local:
            pltpu.make_async_copy(src, dst, sem).start()


    def wait(self, hop):
        whole = self.buffers[hop + 1].at[self.chunk]
        pltpu.make_async_copy(whole, whole, self.sems[1].at[self.first_sem + hop]).wait()

    def wait_sent(self, hop, rows):
        if hop == 0:
            sent = rows.at[:, pl.ds(0, 448), :]
        else:
            sent = self.buffers[hop].at[self.chunk, pl.ds(0, 3)]
        pltpu.make_async_copy(sent, sent, self.sems[0].at[self.first_sem + hop]).wait()


class Gather:
    def __init__(self, me, proj_w, weights, send_sems, recv_sems):
        self.me, self.proj_w, self.weights, self.send_sems, self.recv_sems = me, proj_w, weights, send_sems, recv_sems
        self.x, self.y_lo = me[0], me[1] % 2
        self.mine = self.x * 2 + self.y_lo
        self.columns = pl.ds(pl.multiple_of(me[3] * 384, 128), 384)

    def shard(self, h, first=0, rows=96):
        return self.weights.at[:, pl.ds(pl.multiple_of(h * 96 + first, PIECE), rows), :]

    def part(self, h, first=0, rows=96):
        return self.weights.at[:, pl.ds(pl.multiple_of(h * 96 + first, PIECE), rows), self.columns]

    def copies(self, hop):
        me, x = self.me, self.x
        half = (me[2] % 2) * 48
        if hop == 0:
            for first, step in ((0, 1), (48, 3)):
                yield self.proj_w.at[:, pl.ds(first, 48), self.columns], self.part(self.mine, first, 48), along(1, step)
        elif hop == 1:
            for step in (1, 3, 2):
                for y_lo in range(2):
                    ref = self.part(x * 2 + y_lo, half, 48)
                    yield ref, ref, along(0, step)
        elif hop == 2:
            for other in (1, 2, 3):
                for y_lo, step in ((0, 1), (1, 3)):
                    ref = self.part(((x + other) % 4) * 2 + y_lo, half, 48)
                    yield ref, ref, along(2, step)
        else:
            ref = self.part(x * 2 + 1 - self.y_lo)
            yield ref, ref, (0, 0, 0, 1)
            for other in (1, 2, 3):
                ref = self.part(((x + other) % 4) * 2, 0, 192)
                yield ref, ref, (0, 0, 0, 1)

    def start(self, hop):
        for src, dst, offset in self.copies(hop):
            pltpu.make_async_remote_copy(
                src_ref=src,
                dst_ref=dst,
                send_sem=self.send_sems.at[hop],
                recv_sem=self.recv_sems.at[hop],
                device_id=neighbour(self.me, offset),
                device_id_type=MESH,
            ).start()

    def _wait(self, sems, hop):
        ref = self.weights.at[:, pl.ds(0, (96, 288, 288, 672)[hop]), pl.ds(0, 384)]
        pltpu.make_async_copy(ref, ref, sems.at[hop]).wait()

    def wait(self, hop):
        self._wait(self.recv_sems, hop)

    def wait_sent(self, hop):
        self._wait(self.send_sems, hop)


def each_octet(body):
    def step(m, carry):
        body(m, m // 8, (m // 2) % 4, m % 2)
        return carry

    lax.fori_loop(0, 16, step, 0)


def mix_kernel(
    tokens,
    gain,
    block_w,
    stride_w,
    proj_w,
    scales,
    out,
    out_proj,
    out_scale,
    normed,
    block_v,
    stride_v,
    weights,
    colscale,
    wide,
    rows,
    mixed,
    total,
    fwd0,
    fwd1,
    fwd2,
    fwd3,
    ret0,
    ret1,
    ret2,
    ret3,
    load_sems,
    out_sems,
    send_sems,
    recv_sems,
    gather_send,
    gather_recv,
):
    me = coordinates()
    sems = (send_sems, recv_sems)
    loads = [pltpu.make_async_copy(tokens.at[b], normed.at[b], load_sems.at[b]) for b in range(4)]
    loads.append(pltpu.make_async_copy(block_w, block_v, load_sems.at[4]))
    loads.append(pltpu.make_async_copy(stride_w, stride_v, load_sems.at[5]))
    gather = Gather(me, proj_w, weights, gather_send, gather_recv)
    loads.append(pltpu.make_async_copy(proj_w, gather.shard(gather.mine), load_sems.at[6]))
    for load in loads:
        load.start()
    barrier = pltpu.get_barrier_semaphore()
    for offset in PARTNERS:
        pl.semaphore_signal(barrier, inc=1, device_id=neighbour(me, offset), device_id_type=MESH)

    for b in range(4):
        loads[b].wait()

        def norm(i, carry, b=b):
            r = pl.ds(pl.multiple_of(i * 64, 64), 64)
            x = normed[b, r, :].astype(jnp.float32)
            scale = lax.rsqrt(jnp.mean(x * x, axis=-1, keepdims=True) + 1e-05)
            normed[b, r, :] = (x * scale * gain[...][None, :]).astype(jnp.bfloat16)
            return carry

        lax.fori_loop(0, 8, norm, 0)
    pl.semaphore_wait(barrier, len(PARTNERS))
    gather.start(0)
    loads[4].wait()

    forward = [Journey(me, c, (fwd0, fwd1, fwd2, fwd3), sems, 3 * c) for c in range(CHUNKS)]
    back = [Journey(me, c, (ret0, ret1, ret2, ret3), sems, 3 * (CHUNKS + c)) for c in range(CHUNKS)]

    low = lax.broadcasted_iota(jnp.int32, (8, WIDTH), 0) < 4

    def paired(p, q):
        return jnp.where(low, p, pltpu.roll(q, 4, 0)), jnp.where(low, pltpu.roll(p, 4, 0), q)

    for g in range(CHUNKS // 2):
        for b in range(4):
            x = jnp.dot(block_v[b], normed[b, :, pl.ds(g * 256, 256)], preferred_element_type=jnp.float32)
            for half in range(2):
                wide[half, pl.ds(b, 512, stride=4), :] = x[:, half * WIDTH : (half + 1) * WIDTH]
        for half in range(2):
            chunk = 2 * g + half

            def pack(m, y_hi, z, core, half=half, chunk=chunk):
                for x in range(4):
                    for y_lo in range(2):
                        r = pl.ds(pl.multiple_of((m * 8 + x * 2 + y_lo) * PIECE, PIECE), PIECE)
                        slot = send_slot(ORDERS[chunk], (x, y_hi * 2 + y_lo, z, core))
                        fwd0[(chunk, *slot)] = wide[half, r, :].astype(jnp.bfloat16)

            each_octet(pack)
            forward[chunk].start(0)

    loads[6].wait()
    for hop in range(2):
        gather.wait(hop)
        gather.start(hop + 1)
        for chunk in range(CHUNKS):
            forward[chunk].wait(hop)
            forward[chunk].start(hop + 1)
    loads[5].wait()
    gather.wait(2)
    gather.start(3)

    for chunk in range(CHUNKS):
        forward[chunk].wait(2)

        def split(m, y_hi, z, core, chunk=chunk):
            per_t = [[] for _ in range(4)]
            for x in range(4):
                even, odd = [
                    fwd3[(chunk, *landed_slot(ORDERS[chunk], (x, y_hi * 2 + y_lo, z, core)))].astype(jnp.float32)
                    for y_lo in range(2)
                ]
                for j in range(2):
                    first, second = paired(even[8 * j : 8 * j + 8], odd[8 * j : 8 * j + 8])
                    per_t[2 * j].append(first)
                    per_t[2 * j + 1].append(second)
            r = pl.ds(pl.multiple_of(m * 32, 32), 32)
            for t in range(4):
                rows[t, r, :] = jnp.concatenate(per_t[t], axis=0).astype(jnp.bfloat16)

        each_octet(split)
        for t in range(4):
            mixed[t] = jnp.dot(stride_v[t], rows[t], preferred_element_type=jnp.float32)

        def join(m, y_hi, z, core, chunk=chunk):
            for x in range(4):
                r = pl.ds(pl.multiple_of(m * 32 + x * 8, 8), 8)
                top = paired(mixed[0, r, :], mixed[1, r, :])
                bottom = paired(mixed[2, r, :], mixed[3, r, :])
                for y_lo in range(2):
                    slot = send_slot(ORDERS[chunk], (x, y_hi * 2 + y_lo, z, core))
                    ret0[(chunk, *slot)] = jnp.concatenate([top[y_lo], bottom[y_lo]], axis=0).astype(jnp.bfloat16)

        each_octet(join)
        back[chunk].start(0)

    gather.wait(3)
    for k in range(3):

        def add_squares(i, sums, k=k):
            w = weights[k, pl.ds(pl.multiple_of(i * 64, 64), 64), :].astype(jnp.float32)
            return sums + jnp.sum((w * w).reshape(8, 8, 768), axis=0)

        sums = lax.fori_loop(0, 12, add_squares, jnp.zeros((8, 768), jnp.float32))
        squares = jnp.sum(sums, axis=0, keepdims=True)
        colscale[pl.ds(k, 1), :] = scales[pl.ds(k, 1), :] * lax.rsqrt(squares + 1e-06)
    out_scale[...] = colscale[pl.ds(2, 1), :]
    stores = [pltpu.make_async_copy(weights.at[2], out_proj, out_sems.at[8])]
    stores[0].start()

    def gate_block(i):
        r = pl.ds((i % 2) * 256, 256)
        gate = jnp.dot(normed[i // 2, r, :], weights[1], preferred_element_type=jnp.float32)
        gate = (gate * colscale[pl.ds(1, 1), :]).astype(jnp.bfloat16).astype(jnp.float32)
        gate = gate / (1.0 + jnp.exp(-gate)) * colscale[pl.ds(0, 1), :]
        normed[i // 2, r, :] = gate.astype(jnp.bfloat16)

    for hop in range(2):
        for chunk in range(CHUNKS):
            back[chunk].wait(hop)
            back[chunk].start(hop + 1)
            if hop * CHUNKS + chunk < 8:
                gate_block(hop * CHUNKS + chunk)

    for chunk in range(CHUNKS):
        back[chunk].wait(2)

        def unpack(m, y_hi, z, core, chunk=chunk):
            for x in range(4):
                for y_lo in range(2):
                    r = pl.ds(pl.multiple_of((m % 4) * 128 + (x * 2 + y_lo) * PIECE, PIECE), PIECE)
                    slot = landed_slot(ORDERS[chunk], (x, y_hi * 2 + y_lo, z, core))
                    rows[m // 4, r, :] = ret3[(chunk, *slot)]

        each_octet(unpack)

        def project(i, carry, chunk=chunk):
            left = rows[i // 2, pl.ds(pl.multiple_of((i % 2) * 256, 256), 256), :]
            right = weights[0, pl.ds(chunk * WIDTH, WIDTH), :]
            part = jnp.dot(left, right, preferred_element_type=jnp.float32)
            r = pl.ds(pl.multiple_of(i * 256, 256), 256)
            for n in range(CHUNKS):
                piece = part[:, n * WIDTH : (n + 1) * WIDTH]
                total[n, r, :] = piece if chunk == 0 else total[n, r, :] + piece
            return carry

        if chunk < CHUNKS - 1:
            lax.fori_loop(0, 8, project, 0)
    for i in range(8):
        project(i, 0)
        t = pl.ds(i * 64, 64)
        for n in range(CHUNKS):
            c = pl.ds(n * WIDTH, WIDTH)
            for a in range(4):
                value = total[n, pl.ds(i * 256 + a, 64, stride=4), :]
                normed[a, t, c] = (value * normed[a, t, c].astype(jnp.float32)).astype(jnp.bfloat16)
        stores.append(pltpu.make_async_copy(normed.at[:, t, :], out.at[:, t, :], out_sems.at[i]))
        stores[-1].start()
    for chunk in range(CHUNKS):
        for hop in range(3):
            forward[chunk].wait_sent(hop, rows)
            back[chunk].wait_sent(hop, rows)
    for hop in range(4):
        gather.wait_sent(hop)
    for store in stores:
        store.wait()


def mix(tokens, gain, block_w, stride_w, proj_w, scales):
    sent = (CHUNKS, 4, 2, 4, 4, PIECE, WIDTH)
    half_way = (CHUNKS, 4, 4, 2, 4, PIECE, WIDTH)
    landed = (CHUNKS, 4, 4, 4, 2, PIECE, WIDTH)
    bf16, f32 = jnp.bfloat16, jnp.float32
    hbm, vmem = pl.BlockSpec(memory_space=pl.ANY), pl.BlockSpec(memory_space=pltpu.VMEM)
    return pl.pallas_call(
        mix_kernel,
        out_shape=[
            jax.ShapeDtypeStruct((4, 512, 768), bf16),
            jax.ShapeDtypeStruct((768, 768), bf16),
            jax.ShapeDtypeStruct((1, 768), f32),
        ],
        in_specs=[hbm, vmem, hbm, hbm, hbm, vmem],
        out_specs=[hbm, hbm, vmem],
        scratch_shapes=[
            pltpu.VMEM((4, 512, 768), bf16),
            pltpu.VMEM((4, 512, 512), bf16),
            pltpu.VMEM((4, 512, 512), bf16),
            pltpu.VMEM((3, 768, 768), bf16),
            pltpu.VMEM((3, 768), f32),
            pltpu.VMEM((2, 2048, WIDTH), f32),
            pltpu.VMEM((4, 512, WIDTH), bf16),
            pltpu.VMEM((4, 512, WIDTH), f32),
            pltpu.VMEM((CHUNKS, 2048, WIDTH), f32),
            *[pltpu.VMEM(s, bf16) for s in (sent, sent, half_way, landed)],
            *[pltpu.VMEM(s, bf16) for s in (sent, sent, half_way, landed)],
            pltpu.SemaphoreType.DMA((7,)),
            pltpu.SemaphoreType.DMA((9,)),
            *[pltpu.SemaphoreType.DMA((6 * CHUNKS,)) for _ in range(2)],
            *[pltpu.SemaphoreType.DMA((4,)) for _ in range(2)],
        ],
        compiler_params=pltpu.CompilerParams(collective_id=0, has_side_effects=True, vmem_limit_bytes=56 << 20),
        name="monarch_mix",
    )(tokens, gain, block_w, stride_w, proj_w, scales)


def project_kernel(hidden, weight, scale, out):
    product = jnp.dot(hidden[...], weight[...], preferred_element_type=jnp.float32)
    out[...] = (product * scale[...]).astype(jnp.bfloat16)


def project_out(hidden, weight, scale):
    n, channels = hidden.shape
    return pl.pallas_call(
        project_kernel,
        grid=(n // 256,),
        out_shape=jax.ShapeDtypeStruct((n, channels), jnp.bfloat16),
        in_specs=[
            pl.BlockSpec((256, channels), lambda i: (i, 0)),
            pl.BlockSpec((channels, channels), lambda i: (0, 0)),
            pl.BlockSpec((1, channels), lambda i: (0, 0)),
        ],
        out_specs=pl.BlockSpec((256, channels), lambda i: (i, 0)),
        compiler_params=pltpu.CompilerParams(vmem_limit_bytes=32 << 20),
        name="project_out",
    )(hidden, weight, scale)


def local(tokens, norm_gain, block_weights, stride_weights, proj_weights, proj_scales):
    channels = tokens.shape[-1]
    hidden, out_weight, out_scale = mix(
        tokens.reshape(4, 512, channels), norm_gain, block_weights, stride_weights, proj_weights, proj_scales
    )
    return project_out(hidden.reshape(2048, channels), out_weight, out_scale).reshape(tokens.shape)


def solution(mesh):
    placed = (
        P(None, ("ctx", "chan"), None),
        P(),
        P(("ctx", "chan"), None, None),
        P(("ctx", "chan"), None, None),
        P(None, "chan", None),
        P(),
    )
    return jax.shard_map(
        local, mesh=mesh, in_specs=placed, out_specs=P(None, ("ctx", "chan"), None), check_vma=False
    )
```

```python
import functools

import jax
import jax.numpy as jnp
from jax import lax
from jax.experimental import pallas as pl
from jax.experimental.pallas import tpu as pltpu
from jax.sharding import PartitionSpec as P

MESH = pl.DeviceIdType.MESH
ORDERS = ((0, 1, 2), (1, 2, 0), (2, 0, 1)) * 2
CHUNKS = len(ORDERS)
WIDTH = 128
PIECE = 16


def coordinates():
    c, h = lax.axis_index("ctx"), lax.axis_index("chan")
    return h // 2, (c // 8) * 2 + h % 2, (c // 2) % 4, c % 2


def device_at(x, y, z, k):
    return (y // 2) * 8 + z * 2 + k, x * 2 + y % 2


def neighbour(me, offset):
    x, y, z, k = [(m + o) % n for m, o, n in zip(me, offset, (4, 4, 4, 2))]
    return device_at(x, y, z, k)


def along(axis, step, core=0):
    offset = [0, 0, 0, core]
    offset[axis] = step
    return tuple(offset)


PARTNERS = [along(axis, step, core) for axis in range(3) for step in (1, 3, 2) for core in (0, 1)] + [(0, 0, 0, 1)]


def send_slot(order, point):
    a, b, c = order
    return point[a], point[3], point[b], point[c]


def landed_slot(order, point):
    a, b, c = order
    return point[c], point[b], point[a], point[3]


class Journey:
    def __init__(self, me, chunk, buffers, sems, first_sem):
        self.me, self.chunk, self.buffers, self.sems, self.first_sem = me, chunk, buffers, sems, first_sem

    def copies(self, hop):
        me, chunk = self.me, self.chunk
        axis = ORDERS[chunk][hop]
        source, target = self.buffers[hop], self.buffers[hop + 1]
        here = me[axis]
        send_sem, recv_sem = [s.at[self.first_sem + hop] for s in self.sems]
        local, remote = [], []
        for core in (0, 1) if hop == 0 else (0,):
            for step in (0, 1, 3, 2):
                there = (here + step) % 4
                if hop == 0:
                    src = source.at[chunk, there, (me[3] + core) % 2]
                    dst = target.at[chunk, here, me[3]]
                elif hop == 1:
                    src, dst = source.at[chunk, :, :, there], target.at[chunk, here]
                else:
                    src, dst = source.at[chunk, :, :, :, there], target.at[chunk, here]
                offset = along(axis, step, core)
                if offset == (0, 0, 0, 0):
                    local.append((src, dst, recv_sem))
                else:
                    remote.append((src, dst, send_sem, recv_sem, neighbour(me, offset)))
        return local, remote

    def start(self, hop):
        local, remote = self.copies(hop)
        for src, dst, send_sem, recv_sem, device in remote:
            pltpu.make_async_remote_copy(
                src_ref=src, dst_ref=dst, send_sem=send_sem, recv_sem=recv_sem, device_id=device, device_id_type=MESH
            ).start()
        for src, dst, sem in local:
            pltpu.make_async_copy(src, dst, sem).start()


    def wait(self, hop):
        whole = self.buffers[hop + 1].at[self.chunk]
        pltpu.make_async_copy(whole, whole, self.sems[1].at[self.first_sem + hop]).wait()

    def wait_sent(self, hop, rows):
        if hop == 0:
            sent = rows.at[:, pl.ds(0, 448), :]
        else:
            sent = self.buffers[hop].at[self.chunk, pl.ds(0, 3)]
        pltpu.make_async_copy(sent, sent, self.sems[0].at[self.first_sem + hop]).wait()


class Gather:
    def __init__(self, me, proj_w, weights, send_sems, recv_sems):
        self.me, self.proj_w, self.weights, self.send_sems, self.recv_sems = me, proj_w, weights, send_sems, recv_sems
        self.x, self.y_lo = me[0], me[1] % 2
        self.mine = self.x * 2 + self.y_lo
        self.columns = pl.ds(pl.multiple_of(me[3] * 384, 128), 384)

    def shard(self, h, first=0, rows=96):
        return self.weights.at[:, pl.ds(pl.multiple_of(h * 96 + first, PIECE), rows), :]

    def part(self, h, first=0, rows=96):
        return self.weights.at[:, pl.ds(pl.multiple_of(h * 96 + first, PIECE), rows), self.columns]

    def copies(self, hop):
        me, x = self.me, self.x
        half = (me[2] % 2) * 48
        if hop == 0:
            for first, step in ((0, 1), (48, 3)):
                yield self.proj_w.at[:, pl.ds(first, 48), self.columns], self.part(self.mine, first, 48), along(1, step)
        elif hop == 1:
            for step in (1, 3):
                for y_lo in range(2):
                    ref = self.part(x * 2 + y_lo, half, 48)
                    yield ref, ref, along(0, step)
        elif hop == 2:
            for y_lo, step in ((0, 1), (1, 3)):
                ref = self.part(((x + 4 - step) % 4) * 2 + y_lo, half, 48)
                yield ref, ref, along(0, step)
        elif hop == 3:
            for other in (1, 2, 3):
                for y_lo, step in ((0, 1), (1, 3)):
                    ref = self.part(((x + other) % 4) * 2 + y_lo, half, 48)
                    yield ref, ref, along(2, step)
        else:
            ref = self.part(x * 2 + 1 - self.y_lo)
            yield ref, ref, (0, 0, 0, 1)
            for other in (1, 2, 3):
                ref = self.part(((x + other) % 4) * 2, 0, 192)
                yield ref, ref, (0, 0, 0, 1)

    def start(self, hop):
        for src, dst, offset in self.copies(hop):
            pltpu.make_async_remote_copy(
                src_ref=src,
                dst_ref=dst,
                send_sem=self.send_sems.at[hop],
                recv_sem=self.recv_sems.at[hop],
                device_id=neighbour(self.me, offset),
                device_id_type=MESH,
            ).start()

    def _wait(self, sems, hop):
        ref = self.weights.at[:, pl.ds(0, (96, 192, 96, 288, 672)[hop]), pl.ds(0, 384)]
        pltpu.make_async_copy(ref, ref, sems.at[hop]).wait()

    def wait(self, hop):
        self._wait(self.recv_sems, hop)

    def wait_sent(self, hop):
        self._wait(self.send_sems, hop)


def each_octet(body):
    def step(m, carry):
        body(m, m // 8, (m // 2) % 4, m % 2)
        return carry

    lax.fori_loop(0, 16, step, 0)


def mix_kernel(
    tokens,
    gain,
    block_w,
    stride_w,
    proj_w,
    scales,
    out,
    out_proj,
    out_scale,
    normed,
    block_v,
    stride_v,
    weights,
    colscale,
    wide,
    rows,
    mixed,
    carried,
    total,
    fwd0,
    fwd1,
    fwd2,
    fwd3,
    ret0,
    ret1,
    ret2,
    ret3,
    load_sems,
    out_sems,
    send_sems,
    recv_sems,
    gather_send,
    gather_recv,
):
    me = coordinates()
    sems = (send_sems, recv_sems)
    loads = [pltpu.make_async_copy(tokens.at[b], normed.at[b], load_sems.at[b]) for b in range(4)]
    loads.append(pltpu.make_async_copy(block_w, block_v, load_sems.at[4]))
    loads.append(pltpu.make_async_copy(stride_w, stride_v, load_sems.at[5]))
    gather = Gather(me, proj_w, weights, gather_send, gather_recv)
    loads.append(pltpu.make_async_copy(proj_w, gather.shard(gather.mine), load_sems.at[6]))
    for load in loads:
        load.start()
    barrier = pltpu.get_barrier_semaphore()
    for offset in PARTNERS:
        pl.semaphore_signal(barrier, inc=1, device_id=neighbour(me, offset), device_id_type=MESH)

    for b in range(4):
        loads[b].wait()

        def norm(i, carry, b=b):
            r = pl.ds(pl.multiple_of(i * 64, 64), 64)
            x = normed[b, r, :].astype(jnp.float32)
            scale = lax.rsqrt(jnp.mean(x * x, axis=-1, keepdims=True) + 1e-05)
            normed[b, r, :] = (x * scale * gain[...][None, :]).astype(jnp.bfloat16)
            return carry

        lax.fori_loop(0, 8, norm, 0)
    pl.semaphore_wait(barrier, len(PARTNERS))
    gather.start(0)
    loads[4].wait()

    forward = [Journey(me, c, (fwd0, fwd1, fwd2, fwd3), sems, 3 * c) for c in range(CHUNKS)]
    back = [Journey(me, c, (ret0, ret1, ret2, ret3), sems, 3 * (CHUNKS + c)) for c in range(CHUNKS)]

    low = lax.broadcasted_iota(jnp.int32, (8, WIDTH), 0) < 4

    def paired(p, q):
        return jnp.where(low, p, pltpu.roll(q, 4, 0)), jnp.where(low, pltpu.roll(p, 4, 0), q)

    for g in range(CHUNKS // 2):
        for b in range(4):
            x = jnp.dot(block_v[b], normed[b, :, pl.ds(g * 256, 256)], preferred_element_type=jnp.float32)
            for half in range(2):
                wide[half, pl.ds(b, 512, stride=4), :] = x[:, half * WIDTH : (half + 1) * WIDTH]
        for half in range(2):
            chunk = 2 * g + half

            def pack(m, y_hi, z, core, half=half, chunk=chunk):
                for x in range(4):
                    for y_lo in range(2):
                        r = pl.ds(pl.multiple_of((m * 8 + x * 2 + y_lo) * PIECE, PIECE), PIECE)
                        slot = send_slot(ORDERS[chunk], (x, y_hi * 2 + y_lo, z, core))
                        fwd0[(chunk, *slot)] = wide[half, r, :].astype(jnp.bfloat16)

            each_octet(pack)
            forward[chunk].start(0)

    loads[6].wait()
    gather.wait(0)
    gather.start(1)
    for hop in range(2):
        for chunk in range(CHUNKS):
            forward[chunk].wait(hop)
            forward[chunk].start(hop + 1)
        gather.wait(hop + 1)
        gather.start(hop + 2)
    loads[5].wait()

    for chunk in range(CHUNKS):
        forward[chunk].wait(2)

        def split(m, y_hi, z, core, chunk=chunk):
            per_t = [[] for _ in range(4)]
            for x in range(4):
                even, odd = [
                    fwd3[(chunk, *landed_slot(ORDERS[chunk], (x, y_hi * 2 + y_lo, z, core)))].astype(jnp.float32)
                    for y_lo in range(2)
                ]
                for j in range(2):
                    first, second = paired(even[8 * j : 8 * j + 8], odd[8 * j : 8 * j + 8])
                    per_t[2 * j].append(first)
                    per_t[2 * j + 1].append(second)
            r = pl.ds(pl.multiple_of(m * 32, 32), 32)
            for t in range(4):
                rows[t, r, :] = jnp.concatenate(per_t[t], axis=0).astype(jnp.bfloat16)

        each_octet(split)
        for t in range(4):
            mixed[t] = jnp.dot(stride_v[t], rows[t], preferred_element_type=jnp.float32)

        def join(m, y_hi, z, core, chunk=chunk):
            for x in range(4):
                r = pl.ds(pl.multiple_of(m * 32 + x * 8, 8), 8)
                top = paired(mixed[0, r, :], mixed[1, r, :])
                bottom = paired(mixed[2, r, :], mixed[3, r, :])
                for y_lo in range(2):
                    slot = send_slot(ORDERS[chunk], (x, y_hi * 2 + y_lo, z, core))
                    ret0[(chunk, *slot)] = jnp.concatenate([top[y_lo], bottom[y_lo]], axis=0).astype(jnp.bfloat16)

        each_octet(join)
        back[chunk].start(0)

    gather.wait(3)
    gather.start(4)
    for chunk in range(CHUNKS):
        back[chunk].wait(0)
        back[chunk].start(1)
    gather.wait(4)
    for k in range(3):

        def add_squares(i, sums, k=k):
            w = weights[k, pl.ds(pl.multiple_of(i * 64, 64), 64), :].astype(jnp.float32)
            return sums + jnp.sum((w * w).reshape(8, 8, 768), axis=0)

        sums = lax.fori_loop(0, 12, add_squares, jnp.zeros((8, 768), jnp.float32))
        squares = jnp.sum(sums, axis=0, keepdims=True)
        colscale[pl.ds(k, 1), :] = scales[pl.ds(k, 1), :] * lax.rsqrt(squares + 1e-06)
    out_scale[...] = colscale[pl.ds(2, 1), :]
    stores = [pltpu.make_async_copy(weights.at[2], out_proj, out_sems.at[4])]
    stores[0].start()

    def gate_block(i):
        r = pl.ds((i % 2) * 256, 256)
        gate = jnp.dot(normed[i // 2, r, :], weights[1], preferred_element_type=jnp.float32)
        gate = (gate * colscale[pl.ds(1, 1), :]).astype(jnp.bfloat16).astype(jnp.float32)
        gate = gate / (1.0 + jnp.exp(-gate)) * colscale[pl.ds(0, 1), :]
        normed[i // 2, r, :] = gate.astype(jnp.bfloat16)

    for chunk in range(CHUNKS):
        back[chunk].wait(1)
        back[chunk].start(2)
        for i in ((0, 1), (2, 3), (4,), (5,), (6,), (7,))[chunk]:
            gate_block(i)

    for chunk in range(CHUNKS):
        back[chunk].wait(2)

        def unpack(m, y_hi, z, core, chunk=chunk):
            for x in range(4):
                for y_lo in range(2):
                    r = pl.ds(pl.multiple_of((m * 8 + x * 2 + y_lo) * PIECE, PIECE), PIECE)
                    slot = landed_slot(ORDERS[chunk], (x, y_hi * 2 + y_lo, z, core))
                    wide[chunk % 2, r, :] = ret3[(chunk, *slot)].astype(jnp.float32)

        each_octet(unpack)
        for a in range(4):
            part = wide[chunk % 2, pl.ds(a, 512, stride=4), :].astype(jnp.bfloat16)
            carried[a, :, pl.ds(chunk % 2 * WIDTH, WIDTH)] = part
        if chunk % 2 == 0:
            continue
        right = weights.at[0, pl.ds((chunk - 1) * WIDTH, 2 * WIDTH), :]

        for a in range(4):
            part = jnp.dot(carried[a], right[...], preferred_element_type=jnp.float32)
            if chunk == 1:
                total[a] = part
            elif chunk < CHUNKS - 1:
                total[a] = total[a] + part
            else:
                part = (total[a] + part) * normed[a].astype(jnp.float32)
                normed[a] = part.astype(jnp.bfloat16)
                stores.append(pltpu.make_async_copy(normed.at[a], out.at[a], out_sems.at[a]))
                stores[-1].start()
    for chunk in range(CHUNKS):
        for hop in range(3):
            forward[chunk].wait_sent(hop, rows)
            back[chunk].wait_sent(hop, rows)
    for hop in range(5):
        gather.wait_sent(hop)
    for store in stores:
        store.wait()


def mix(tokens, gain, block_w, stride_w, proj_w, scales):
    sent = (CHUNKS, 4, 2, 4, 4, PIECE, WIDTH)
    half_way = (CHUNKS, 4, 4, 2, 4, PIECE, WIDTH)
    landed = (CHUNKS, 4, 4, 4, 2, PIECE, WIDTH)
    bf16, f32 = jnp.bfloat16, jnp.float32
    hbm, vmem = pl.BlockSpec(memory_space=pl.ANY), pl.BlockSpec(memory_space=pltpu.VMEM)
    return pl.pallas_call(
        mix_kernel,
        out_shape=[
            jax.ShapeDtypeStruct((4, 512, 768), bf16),
            jax.ShapeDtypeStruct((768, 768), bf16),
            jax.ShapeDtypeStruct((1, 768), f32),
        ],
        in_specs=[hbm, vmem, hbm, hbm, hbm, vmem],
        out_specs=[hbm, hbm, vmem],
        scratch_shapes=[
            pltpu.VMEM((4, 512, 768), bf16),
            pltpu.VMEM((4, 512, 512), bf16),
            pltpu.VMEM((4, 512, 512), bf16),
            pltpu.VMEM((3, 768, 768), bf16),
            pltpu.VMEM((3, 768), f32),
            pltpu.VMEM((2, 2048, WIDTH), f32),
            pltpu.VMEM((4, 512, WIDTH), bf16),
            pltpu.VMEM((4, 512, WIDTH), f32),
            pltpu.VMEM((4, 512, 2 * WIDTH), bf16),
            pltpu.VMEM((4, 512, 768), f32),
            *[pltpu.VMEM(s, bf16) for s in (sent, sent, half_way, landed)],
            *[pltpu.VMEM(s, bf16) for s in (sent, sent, half_way, landed)],
            pltpu.SemaphoreType.DMA((7,)),
            pltpu.SemaphoreType.DMA((5,)),
            *[pltpu.SemaphoreType.DMA((6 * CHUNKS,)) for _ in range(2)],
            *[pltpu.SemaphoreType.DMA((5,)) for _ in range(2)],
        ],
        compiler_params=pltpu.CompilerParams(collective_id=0, has_side_effects=True, vmem_limit_bytes=56 << 20),
        name="monarch_mix",
    )(tokens, gain, block_w, stride_w, proj_w, scales)


def project_kernel(hidden, weight, scale, out):
    product = jnp.dot(hidden[...], weight[...], preferred_element_type=jnp.float32)
    out[...] = (product * scale[...]).astype(jnp.bfloat16)


def project_out(hidden, weight, scale):
    n, channels = hidden.shape
    return pl.pallas_call(
        project_kernel,
        grid=(n // 256,),
        out_shape=jax.ShapeDtypeStruct((n, channels), jnp.bfloat16),
        in_specs=[
            pl.BlockSpec((256, channels), lambda i: (i, 0)),
            pl.BlockSpec((channels, channels), lambda i: (0, 0)),
            pl.BlockSpec((1, channels), lambda i: (0, 0)),
        ],
        out_specs=pl.BlockSpec((256, channels), lambda i: (i, 0)),
        compiler_params=pltpu.CompilerParams(vmem_limit_bytes=60 << 20),
        name="project_out",
    )(hidden, weight, scale)


def local(tokens, norm_gain, block_weights, stride_weights, proj_weights, proj_scales):
    channels = tokens.shape[-1]
    hidden, out_weight, out_scale = mix(
        tokens.reshape(4, 512, channels), norm_gain, block_weights, stride_weights, proj_weights, proj_scales
    )
    return project_out(hidden.reshape(2048, channels), out_weight, out_scale).reshape(tokens.shape)


def solution(mesh):
    placed = (
        P(None, ("ctx", "chan"), None),
        P(),
        P(("ctx", "chan"), None, None),
        P(("ctx", "chan"), None, None),
        P(None, "chan", None),
        P(),
    )
    return jax.shard_map(
        local, mesh=mesh, in_specs=placed, out_specs=P(None, ("ctx", "chan"), None), check_vma=False
    )
```

```python
import functools

import jax
import jax.numpy as jnp
from jax import lax
from jax.experimental import pallas as pl
from jax.experimental.pallas import tpu as pltpu
from jax.sharding import PartitionSpec as P

MESH = pl.DeviceIdType.MESH
ORDERS = ((0, 1, 2), (1, 2, 0), (2, 0, 1)) * 2
CHUNKS = len(ORDERS)
WIDTH = 128
PIECE = 16


def coordinates():
    c, h = lax.axis_index("ctx"), lax.axis_index("chan")
    return h // 2, (c // 8) * 2 + h % 2, (c // 2) % 4, c % 2


def device_at(x, y, z, k):
    return (y // 2) * 8 + z * 2 + k, x * 2 + y % 2


def neighbour(me, offset):
    x, y, z, k = [(m + o) % n for m, o, n in zip(me, offset, (4, 4, 4, 2))]
    return device_at(x, y, z, k)


def along(axis, step, core=0):
    offset = [0, 0, 0, core]
    offset[axis] = step
    return tuple(offset)


PARTNERS = [along(axis, step, core) for axis in range(3) for step in (1, 3, 2) for core in (0, 1)] + [(0, 0, 0, 1)]


def send_slot(order, point):
    a, b, c = order
    return point[a], point[3], point[b], point[c]


def landed_slot(order, point):
    a, b, c = order
    return point[c], point[b], point[a], point[3]


class Journey:
    def __init__(self, me, chunk, buffers, sems, first_sem):
        self.me, self.chunk, self.buffers, self.sems, self.first_sem = me, chunk, buffers, sems, first_sem

    def copies(self, hop):
        me, chunk = self.me, self.chunk
        axis = ORDERS[chunk][hop]
        source, target = self.buffers[hop], self.buffers[hop + 1]
        here = me[axis]
        send_sem, recv_sem = [s.at[self.first_sem + hop] for s in self.sems]
        local, remote = [], []
        for core in (0, 1) if hop == 0 else (0,):
            for step in (0, 1, 3, 2):
                there = (here + step) % 4
                if hop == 0:
                    src = source.at[chunk, there, (me[3] + core) % 2]
                    dst = target.at[chunk, here, me[3]]
                elif hop == 1:
                    src, dst = source.at[chunk, :, :, there], target.at[chunk, here]
                else:
                    src, dst = source.at[chunk, :, :, :, there], target.at[chunk, here]
                offset = along(axis, step, core)
                if offset == (0, 0, 0, 0):
                    local.append((src, dst, recv_sem))
                else:
                    remote.append((src, dst, send_sem, recv_sem, neighbour(me, offset)))
        return local, remote

    def start(self, hop):
        local, remote = self.copies(hop)
        for src, dst, send_sem, recv_sem, device in remote:
            pltpu.make_async_remote_copy(
                src_ref=src, dst_ref=dst, send_sem=send_sem, recv_sem=recv_sem, device_id=device, device_id_type=MESH
            ).start()
        for src, dst, sem in local:
            pltpu.make_async_copy(src, dst, sem).start()


    def wait(self, hop):
        whole = self.buffers[hop + 1].at[self.chunk]
        pltpu.make_async_copy(whole, whole, self.sems[1].at[self.first_sem + hop]).wait()

    def wait_sent(self, hop, rows):
        if hop == 0:
            sent = rows.at[:, pl.ds(0, 448), :]
        else:
            sent = self.buffers[hop].at[self.chunk, pl.ds(0, 3)]
        pltpu.make_async_copy(sent, sent, self.sems[0].at[self.first_sem + hop]).wait()


class Gather:
    def __init__(self, me, proj_w, weights, send_sems, recv_sems):
        self.me, self.proj_w, self.weights, self.send_sems, self.recv_sems = me, proj_w, weights, send_sems, recv_sems
        self.x, self.y_lo = me[0], me[1] % 2
        self.mine = self.x * 2 + self.y_lo
        self.columns = pl.ds(pl.multiple_of(me[3] * 384, 128), 384)

    def shard(self, h, first=0, rows=96):
        return self.weights.at[:, pl.ds(pl.multiple_of(h * 96 + first, PIECE), rows), :]

    def part(self, h, first=0, rows=96):
        return self.weights.at[:, pl.ds(pl.multiple_of(h * 96 + first, PIECE), rows), self.columns]

    def copies(self, hop):
        me, x = self.me, self.x
        half = (me[2] % 2) * 48
        if hop == 0:
            for first, step in ((0, 1), (48, 3)):
                yield self.proj_w.at[:, pl.ds(first, 48), self.columns], self.part(self.mine, first, 48), along(1, step)
        elif hop == 1:
            for step in (1, 3):
                for y_lo in range(2):
                    ref = self.part(x * 2 + y_lo, half, 48)
                    yield ref, ref, along(0, step)
        elif hop == 2:
            for y_lo, step in ((0, 1), (1, 3)):
                ref = self.part(((x + 4 - step) % 4) * 2 + y_lo, half, 48)
                yield ref, ref, along(0, step)
        elif hop == 3:
            for other in (1, 2, 3):
                for y_lo, step in ((0, 1), (1, 3)):
                    ref = self.part(((x + other) % 4) * 2 + y_lo, half, 48)
                    yield ref, ref, along(2, step)
        else:
            ref = self.part(x * 2 + 1 - self.y_lo)
            yield ref, ref, (0, 0, 0, 1)
            for other in (1, 2, 3):
                ref = self.part(((x + other) % 4) * 2, 0, 192)
                yield ref, ref, (0, 0, 0, 1)

    def start(self, hop):
        for src, dst, offset in self.copies(hop):
            pltpu.make_async_remote_copy(
                src_ref=src,
                dst_ref=dst,
                send_sem=self.send_sems.at[hop],
                recv_sem=self.recv_sems.at[hop],
                device_id=neighbour(self.me, offset),
                device_id_type=MESH,
            ).start()

    def _wait(self, sems, hop):
        ref = self.weights.at[:, pl.ds(0, (96, 192, 96, 288, 672)[hop]), pl.ds(0, 384)]
        pltpu.make_async_copy(ref, ref, sems.at[hop]).wait()

    def wait(self, hop):
        self._wait(self.recv_sems, hop)

    def wait_sent(self, hop):
        self._wait(self.send_sems, hop)


def each_octet(body):
    def step(m, carry):
        body(m, m // 8, (m // 2) % 4, m % 2)
        return carry

    lax.fori_loop(0, 16, step, 0)


def mix_kernel(
    tokens,
    gain,
    block_w,
    stride_w,
    proj_w,
    scales,
    out,
    out_proj,
    out_scale,
    normed,
    block_v,
    stride_v,
    weights,
    colscale,
    wide,
    rows,
    mixed,
    carried,
    total,
    fwd0,
    fwd1,
    fwd2,
    fwd3,
    ret0,
    ret1,
    ret2,
    ret3,
    load_sems,
    out_sems,
    send_sems,
    recv_sems,
    gather_send,
    gather_recv,
):
    me = coordinates()
    sems = (send_sems, recv_sems)
    loads = [pltpu.make_async_copy(tokens.at[b], normed.at[b], load_sems.at[b]) for b in range(4)]
    loads.append(pltpu.make_async_copy(block_w, block_v, load_sems.at[4]))
    loads.append(pltpu.make_async_copy(stride_w, stride_v, load_sems.at[5]))
    gather = Gather(me, proj_w, weights, gather_send, gather_recv)
    loads.append(pltpu.make_async_copy(proj_w, gather.shard(gather.mine), load_sems.at[6]))
    for load in loads:
        load.start()
    barrier = pltpu.get_barrier_semaphore()
    for offset in PARTNERS:
        pl.semaphore_signal(barrier, inc=1, device_id=neighbour(me, offset), device_id_type=MESH)

    for b in range(4):
        loads[b].wait()

        def norm(i, carry, b=b):
            r = pl.ds(pl.multiple_of(i * 64, 64), 64)
            x = normed[b, r, :].astype(jnp.float32)
            scale = lax.rsqrt(jnp.mean(x * x, axis=-1, keepdims=True) + 1e-05)
            normed[b, r, :] = (x * scale * gain[...][None, :]).astype(jnp.bfloat16)
            return carry

        lax.fori_loop(0, 8, norm, 0)
    pl.semaphore_wait(barrier, len(PARTNERS))
    gather.start(0)
    loads[4].wait()

    forward = [Journey(me, c, (fwd0, fwd1, fwd2, fwd3), sems, 3 * c) for c in range(CHUNKS)]
    back = [Journey(me, c, (ret0, ret1, ret2, ret3), sems, 3 * (CHUNKS + c)) for c in range(CHUNKS)]

    low = lax.broadcasted_iota(jnp.int32, (8, WIDTH), 0) < 4

    def paired(p, q):
        return jnp.where(low, p, pltpu.roll(q, 4, 0)), jnp.where(low, pltpu.roll(p, 4, 0), q)

    for g in range(CHUNKS // 2):
        for b in range(4):
            x = jnp.dot(block_v[b], normed[b, :, pl.ds(g * 256, 256)], preferred_element_type=jnp.float32)
            for half in range(2):
                wide[half, pl.ds(b, 512, stride=4), :] = x[:, half * WIDTH : (half + 1) * WIDTH]
        for half in range(2):
            chunk = 2 * g + half

            def pack(m, y_hi, z, core, half=half, chunk=chunk):
                for x in range(4):
                    for y_lo in range(2):
                        r = pl.ds(pl.multiple_of((m * 8 + x * 2 + y_lo) * PIECE, PIECE), PIECE)
                        slot = send_slot(ORDERS[chunk], (x, y_hi * 2 + y_lo, z, core))
                        fwd0[(chunk, *slot)] = wide[half, r, :].astype(jnp.bfloat16)

            each_octet(pack)
            forward[chunk].start(0)

    loads[6].wait()
    gather.wait(0)
    gather.start(1)
    for hop in range(2):
        for chunk in range(CHUNKS):
            forward[chunk].wait(hop)
            forward[chunk].start(hop + 1)
        gather.wait(hop + 1)
        gather.start(hop + 2)
    loads[5].wait()

    for chunk in range(CHUNKS):
        forward[chunk].wait(2)

        def split(m, y_hi, z, core, chunk=chunk):
            per_t = [[] for _ in range(4)]
            for x in range(4):
                even, odd = [
                    fwd3[(chunk, *landed_slot(ORDERS[chunk], (x, y_hi * 2 + y_lo, z, core)))].astype(jnp.float32)
                    for y_lo in range(2)
                ]
                for j in range(2):
                    first, second = paired(even[8 * j : 8 * j + 8], odd[8 * j : 8 * j + 8])
                    per_t[2 * j].append(first)
                    per_t[2 * j + 1].append(second)
            r = pl.ds(pl.multiple_of(m * 32, 32), 32)
            for t in range(4):
                rows[t, r, :] = jnp.concatenate(per_t[t], axis=0).astype(jnp.bfloat16)

        each_octet(split)
        for t in range(4):
            mixed[t] = jnp.dot(stride_v[t], rows[t], preferred_element_type=jnp.float32)

        def join(m, y_hi, z, core, chunk=chunk):
            for x in range(4):
                r = pl.ds(pl.multiple_of(m * 32 + x * 8, 8), 8)
                top = paired(mixed[0, r, :], mixed[1, r, :])
                bottom = paired(mixed[2, r, :], mixed[3, r, :])
                for y_lo in range(2):
                    slot = send_slot(ORDERS[chunk], (x, y_hi * 2 + y_lo, z, core))
                    ret0[(chunk, *slot)] = jnp.concatenate([top[y_lo], bottom[y_lo]], axis=0).astype(jnp.bfloat16)

        each_octet(join)
        back[chunk].start(0)

    gather.wait(3)
    gather.start(4)
    for chunk in range(CHUNKS):
        back[chunk].wait(0)
        back[chunk].start(1)
    gather.wait(4)
    for k in range(3):

        def add_squares(i, sums, k=k):
            w = weights[k, pl.ds(pl.multiple_of(i * 64, 64), 64), :].astype(jnp.float32)
            return sums + jnp.sum((w * w).reshape(8, 8, 768), axis=0)

        sums = lax.fori_loop(0, 12, add_squares, jnp.zeros((8, 768), jnp.float32))
        squares = jnp.sum(sums, axis=0, keepdims=True)
        colscale[pl.ds(k, 1), :] = scales[pl.ds(k, 1), :] * lax.rsqrt(squares + 1e-06)
    out_scale[...] = colscale[pl.ds(2, 1), :]
    stores = [pltpu.make_async_copy(weights.at[2], out_proj, out_sems.at[4])]
    stores[0].start()

    def gate_block(i):
        r = pl.ds((i % 2) * 256, 256)
        gate = jnp.dot(normed[i // 2, r, :], weights[1], preferred_element_type=jnp.float32)
        gate = (gate * colscale[pl.ds(1, 1), :]).astype(jnp.bfloat16).astype(jnp.float32)
        gate = gate / (1.0 + jnp.exp(-gate)) * colscale[pl.ds(0, 1), :]
        normed[i // 2, r, :] = gate.astype(jnp.bfloat16)

    for chunk in range(CHUNKS):
        back[chunk].wait(1)
        back[chunk].start(2)
        for i in ((0, 1), (2, 3), (4,), (5,), (6,), (7,))[chunk]:
            gate_block(i)

    for chunk in range(CHUNKS):
        back[chunk].wait(2)

        def unpack(m, y_hi, z, core, chunk=chunk):
            for x in range(4):
                for y_lo in range(2):
                    r = pl.ds(pl.multiple_of((m * 8 + x * 2 + y_lo) * PIECE, PIECE), PIECE)
                    slot = landed_slot(ORDERS[chunk], (x, y_hi * 2 + y_lo, z, core))
                    wide[chunk % 2, r, :] = ret3[(chunk, *slot)].astype(jnp.float32)

        each_octet(unpack)
        for a in range(4):
            part = wide[chunk % 2, pl.ds(a, 512, stride=4), :].astype(jnp.bfloat16)
            carried[a, :, pl.ds(chunk % 2 * WIDTH, WIDTH)] = part
        if chunk % 2 == 0:
            continue
        right = weights.at[0, pl.ds((chunk - 1) * WIDTH, 2 * WIDTH), :]

        for a in range(4):
            part = jnp.dot(carried[a], right[...], preferred_element_type=jnp.float32)
            if chunk == 1:
                total[a] = part
            elif chunk < CHUNKS - 1:
                total[a] = total[a] + part
            else:
                part = (total[a] + part) * normed[a].astype(jnp.float32)
                normed[a] = part.astype(jnp.bfloat16)
                stores.append(pltpu.make_async_copy(normed.at[a], out.at[a], out_sems.at[a]))
                stores[-1].start()
    for chunk in range(CHUNKS):
        for hop in range(3):
            forward[chunk].wait_sent(hop, rows)
            back[chunk].wait_sent(hop, rows)
    for hop in range(5):
        gather.wait_sent(hop)
    for store in stores:
        store.wait()


def mix(tokens, gain, block_w, stride_w, proj_w, scales):
    sent = (CHUNKS, 4, 2, 4, 4, PIECE, WIDTH)
    half_way = (CHUNKS, 4, 4, 2, 4, PIECE, WIDTH)
    landed = (CHUNKS, 4, 4, 4, 2, PIECE, WIDTH)
    bf16, f32 = jnp.bfloat16, jnp.float32
    hbm, vmem = pl.BlockSpec(memory_space=pl.ANY), pl.BlockSpec(memory_space=pltpu.VMEM)
    return pl.pallas_call(
        mix_kernel,
        out_shape=[
            pltpu.VMEM((4, 512, 768), bf16),
            pltpu.VMEM((768, 768), bf16),
            pltpu.VMEM((1, 768), f32),
        ],
        in_specs=[hbm, vmem, hbm, hbm, hbm, vmem],
        out_specs=[hbm, hbm, vmem],
        scratch_shapes=[
            pltpu.VMEM((4, 512, 768), bf16),
            pltpu.VMEM((4, 512, 512), bf16),
            pltpu.VMEM((4, 512, 512), bf16),
            pltpu.VMEM((3, 768, 768), bf16),
            pltpu.VMEM((3, 768), f32),
            pltpu.VMEM((2, 2048, WIDTH), f32),
            pltpu.VMEM((4, 512, WIDTH), bf16),
            pltpu.VMEM((4, 512, WIDTH), f32),
            pltpu.VMEM((4, 512, 2 * WIDTH), bf16),
            pltpu.VMEM((4, 512, 768), f32),
            *[pltpu.VMEM(s, bf16) for s in (sent, sent, half_way, landed)],
            *[pltpu.VMEM(s, bf16) for s in (sent, sent, half_way, landed)],
            pltpu.SemaphoreType.DMA((7,)),
            pltpu.SemaphoreType.DMA((5,)),
            *[pltpu.SemaphoreType.DMA((6 * CHUNKS,)) for _ in range(2)],
            *[pltpu.SemaphoreType.DMA((5,)) for _ in range(2)],
        ],
        compiler_params=pltpu.CompilerParams(collective_id=0, has_side_effects=True, vmem_limit_bytes=52 << 20),
        name="monarch_mix",
    )(tokens, gain, block_w, stride_w, proj_w, scales)


def project_kernel(hidden, weight, scale, out, result, sems):
    stores = []
    for i in range(4):
        product = jnp.dot(hidden[i], weight[...], preferred_element_type=jnp.float32)
        result[i] = (product * scale[...]).astype(jnp.bfloat16)
        stores.append(pltpu.make_async_copy(result.at[i], out.at[i], sems.at[i]))
        stores[-1].start()
    for store in stores:
        store.wait()


def project_out(hidden, weight, scale):
    vmem = pl.BlockSpec(memory_space=pltpu.VMEM)
    return pl.pallas_call(
        project_kernel,
        out_shape=jax.ShapeDtypeStruct(hidden.shape, jnp.bfloat16),
        in_specs=[vmem, vmem, vmem],
        out_specs=pl.BlockSpec(memory_space=pl.ANY),
        scratch_shapes=[pltpu.VMEM(hidden.shape, jnp.bfloat16), pltpu.SemaphoreType.DMA((4,))],
        compiler_params=pltpu.CompilerParams(vmem_limit_bytes=24 << 20),
        name="project_out",
    )(
        pltpu.with_memory_space_constraint(hidden, pltpu.VMEM),
        pltpu.with_memory_space_constraint(weight, pltpu.VMEM),
        pltpu.with_memory_space_constraint(scale, pltpu.VMEM),
    )


def local(tokens, norm_gain, block_weights, stride_weights, proj_weights, proj_scales):
    channels = tokens.shape[-1]
    hidden, out_weight, out_scale = mix(
        tokens.reshape(4, 512, channels), norm_gain, block_weights, stride_weights, proj_weights, proj_scales
    )
    return project_out(hidden, out_weight, out_scale).reshape(tokens.shape)


def solution(mesh):
    placed = (
        P(None, ("ctx", "chan"), None),
        P(),
        P(("ctx", "chan"), None, None),
        P(("ctx", "chan"), None, None),
        P(None, "chan", None),
        P(),
    )
    return jax.shard_map(
        local, mesh=mesh, in_specs=placed, out_specs=P(None, ("ctx", "chan"), None), check_vma=False
    )
```

```python
import functools

import jax
import jax.numpy as jnp
from jax import lax
from jax.experimental import pallas as pl
from jax.experimental.pallas import tpu as pltpu
from jax.sharding import PartitionSpec as P

MESH = pl.DeviceIdType.MESH
ORDERS = ((0, 1, 2), (1, 2, 0), (2, 0, 1)) * 2
CHUNKS = len(ORDERS)
WIDTH = 128
PIECE = 16


def coordinates():
    c, h = lax.axis_index("ctx"), lax.axis_index("chan")
    return h // 2, (c // 8) * 2 + h % 2, (c // 2) % 4, c % 2


def device_at(x, y, z, k):
    return (y // 2) * 8 + z * 2 + k, x * 2 + y % 2


def neighbour(me, offset):
    x, y, z, k = [(m + o) % n for m, o, n in zip(me, offset, (4, 4, 4, 2))]
    return device_at(x, y, z, k)


def along(axis, step, core=0):
    offset = [0, 0, 0, core]
    offset[axis] = step
    return tuple(offset)


PARTNERS = [along(axis, step, core) for axis in range(3) for step in (1, 3, 2) for core in (0, 1)] + [(0, 0, 0, 1)]


def send_slot(order, point):
    a, b, c = order
    return point[a], point[3], point[b], point[c]


def landed_slot(order, point):
    a, b, c = order
    return point[c], point[b], point[a], point[3]


class Journey:
    def __init__(self, me, chunk, buffers, sems, first_sem):
        self.me, self.chunk, self.buffers, self.sems, self.first_sem = me, chunk, buffers, sems, first_sem

    def copies(self, hop):
        me, chunk = self.me, self.chunk
        axis = ORDERS[chunk][hop]
        source, target = self.buffers[hop], self.buffers[hop + 1]
        here = me[axis]
        send_sem, recv_sem = [s.at[self.first_sem + hop] for s in self.sems]
        local, remote = [], []
        for core in (0, 1) if hop == 0 else (0,):
            for step in (0, 1, 3, 2):
                there = (here + step) % 4
                if hop == 0:
                    src = source.at[chunk, there, (me[3] + core) % 2]
                    dst = target.at[chunk, here, me[3]]
                elif hop == 1:
                    src, dst = source.at[chunk, :, :, there], target.at[chunk, here]
                else:
                    src, dst = source.at[chunk, :, :, :, there], target.at[chunk, here]
                offset = along(axis, step, core)
                if offset == (0, 0, 0, 0):
                    local.append((src, dst, recv_sem))
                else:
                    remote.append((src, dst, send_sem, recv_sem, neighbour(me, offset)))
        return local, remote

    def start(self, hop):
        local, remote = self.copies(hop)
        for src, dst, send_sem, recv_sem, device in remote:
            pltpu.make_async_remote_copy(
                src_ref=src, dst_ref=dst, send_sem=send_sem, recv_sem=recv_sem, device_id=device, device_id_type=MESH
            ).start()
        for src, dst, sem in local:
            pltpu.make_async_copy(src, dst, sem).start()


    def wait(self, hop):
        whole = self.buffers[hop + 1].at[self.chunk]
        pltpu.make_async_copy(whole, whole, self.sems[1].at[self.first_sem + hop]).wait()

    def wait_sent(self, hop, rows):
        if hop == 0:
            sent = rows.at[:, pl.ds(0, 448), :]
        else:
            sent = self.buffers[hop].at[self.chunk, pl.ds(0, 3)]
        pltpu.make_async_copy(sent, sent, self.sems[0].at[self.first_sem + hop]).wait()


class Gather:
    def __init__(self, me, proj_w, weights, send_sems, recv_sems):
        self.me, self.proj_w, self.weights, self.send_sems, self.recv_sems = me, proj_w, weights, send_sems, recv_sems
        self.x, self.y_lo = me[0], me[1] % 2
        self.mine = self.x * 2 + self.y_lo
        self.columns = pl.ds(pl.multiple_of(me[3] * 384, 128), 384)

    def shard(self, h, first=0, rows=96):
        return self.weights.at[:, pl.ds(pl.multiple_of(h * 96 + first, PIECE), rows), :]

    def part(self, h, first=0, rows=96):
        return self.weights.at[:, pl.ds(pl.multiple_of(h * 96 + first, PIECE), rows), self.columns]

    def copies(self, hop):
        me, x = self.me, self.x
        half = (me[2] % 2) * 48
        if hop == 0:
            for first, step in ((0, 1), (48, 3)):
                yield self.proj_w.at[:, pl.ds(first, 48), self.columns], self.part(self.mine, first, 48), along(1, step)
        elif hop == 1:
            for step in (1, 3):
                for y_lo in range(2):
                    ref = self.part(x * 2 + y_lo, half, 48)
                    yield ref, ref, along(0, step)
        elif hop == 2:
            for y_lo, step in ((0, 1), (1, 3)):
                ref = self.part(((x + 4 - step) % 4) * 2 + y_lo, half, 48)
                yield ref, ref, along(0, step)
        elif hop == 3:
            for other in (1, 2, 3):
                for y_lo, step in ((0, 1), (1, 3)):
                    ref = self.part(((x + other) % 4) * 2 + y_lo, half, 48)
                    yield ref, ref, along(2, step)
        else:
            ref = self.part(x * 2 + 1 - self.y_lo)
            yield ref, ref, (0, 0, 0, 1)
            for other in (1, 2, 3):
                ref = self.part(((x + other) % 4) * 2, 0, 192)
                yield ref, ref, (0, 0, 0, 1)

    def start(self, hop):
        for src, dst, offset in self.copies(hop):
            pltpu.make_async_remote_copy(
                src_ref=src,
                dst_ref=dst,
                send_sem=self.send_sems.at[hop],
                recv_sem=self.recv_sems.at[hop],
                device_id=neighbour(self.me, offset),
                device_id_type=MESH,
            ).start()

    def _wait(self, sems, hop):
        ref = self.weights.at[:, pl.ds(0, (96, 192, 96, 288, 672)[hop]), pl.ds(0, 384)]
        pltpu.make_async_copy(ref, ref, sems.at[hop]).wait()

    def wait(self, hop):
        self._wait(self.recv_sems, hop)

    def wait_sent(self, hop):
        self._wait(self.send_sems, hop)


def each_octet(body):
    def step(m, carry):
        body(m, m // 8, (m // 2) % 4, m % 2)
        return carry

    lax.fori_loop(0, 16, step, 0)


def mix_kernel(
    tokens,
    gain,
    block_w,
    stride_w,
    proj_w,
    scales,
    out,
    out_proj,
    out_scale,
    normed,
    block_v,
    stride_v,
    weights,
    colscale,
    wide,
    rows,
    mixed,
    carried,
    total,
    fwd0,
    fwd1,
    fwd2,
    fwd3,
    ret0,
    ret1,
    ret2,
    ret3,
    load_sems,
    out_sems,
    send_sems,
    recv_sems,
    gather_send,
    gather_recv,
):
    me = coordinates()
    sems = (send_sems, recv_sems)
    loads = [pltpu.make_async_copy(tokens.at[b], normed.at[b], load_sems.at[b]) for b in range(4)]
    loads.append(pltpu.make_async_copy(block_w, block_v, load_sems.at[4]))
    loads.append(pltpu.make_async_copy(stride_w, stride_v, load_sems.at[5]))
    gather = Gather(me, proj_w, weights, gather_send, gather_recv)
    loads.append(pltpu.make_async_copy(proj_w, gather.shard(gather.mine), load_sems.at[6]))
    for load in loads:
        load.start()
    barrier = pltpu.get_barrier_semaphore()
    for offset in PARTNERS:
        pl.semaphore_signal(barrier, inc=1, device_id=neighbour(me, offset), device_id_type=MESH)

    pl.semaphore_wait(barrier, len(PARTNERS))
    gather.start(0)
    for b in range(4):
        loads[b].wait()

        def norm(i, carry, b=b):
            r = pl.ds(pl.multiple_of(i * 64, 64), 64)
            x = normed[b, r, :].astype(jnp.float32)
            scale = lax.rsqrt(jnp.mean(x * x, axis=-1, keepdims=True) + 1e-05)
            normed[b, r, :] = (x * scale * gain[...][None, :]).astype(jnp.bfloat16)
            return carry

        lax.fori_loop(0, 8, norm, 0)
    loads[4].wait()

    forward = [Journey(me, c, (fwd0, fwd1, fwd2, fwd3), sems, 3 * c) for c in range(CHUNKS)]
    back = [Journey(me, c, (ret0, ret1, ret2, ret3), sems, 3 * (CHUNKS + c)) for c in range(CHUNKS)]

    low = lax.broadcasted_iota(jnp.int32, (8, WIDTH), 0) < 4

    def paired(p, q):
        return jnp.where(low, p, pltpu.roll(q, 4, 0)), jnp.where(low, pltpu.roll(p, 4, 0), q)

    for first, count in ((0, 2), (2, 1), (3, 1), (4, 2)):
        if first == 3:
            loads[6].wait()
            gather.wait(0)
            gather.start(1)
        for b in range(4):
            columns = pl.ds(first * WIDTH, count * WIDTH)
            x = jnp.dot(block_v[b], normed[b, :, columns], preferred_element_type=jnp.float32)
            for half in range(count):
                wide[half, pl.ds(b, 512, stride=4), :] = x[:, half * WIDTH : (half + 1) * WIDTH]
        for half in range(count):
            chunk = first + half

            def pack(m, y_hi, z, core, half=half, chunk=chunk):
                for x in range(4):
                    for y_lo in range(2):
                        r = pl.ds(pl.multiple_of((m * 8 + x * 2 + y_lo) * PIECE, PIECE), PIECE)
                        slot = send_slot(ORDERS[chunk], (x, y_hi * 2 + y_lo, z, core))
                        fwd0[(chunk, *slot)] = wide[half, r, :].astype(jnp.bfloat16)

            each_octet(pack)
            forward[chunk].start(0)

    for hop in range(2):
        for chunk in range(CHUNKS):
            forward[chunk].wait(hop)
            forward[chunk].start(hop + 1)
        gather.wait(hop + 1)
        gather.start(hop + 2)
    loads[5].wait()

    for chunk in range(CHUNKS):
        forward[chunk].wait(2)

        def split(m, y_hi, z, core, chunk=chunk):
            per_t = [[] for _ in range(4)]
            for x in range(4):
                even, odd = [
                    fwd3[(chunk, *landed_slot(ORDERS[chunk], (x, y_hi * 2 + y_lo, z, core)))].astype(jnp.float32)
                    for y_lo in range(2)
                ]
                for j in range(2):
                    first, second = paired(even[8 * j : 8 * j + 8], odd[8 * j : 8 * j + 8])
                    per_t[2 * j].append(first)
                    per_t[2 * j + 1].append(second)
            r = pl.ds(pl.multiple_of(m * 32, 32), 32)
            for t in range(4):
                rows[t, r, :] = jnp.concatenate(per_t[t], axis=0).astype(jnp.bfloat16)

        each_octet(split)
        for t in range(4):
            mixed[t] = jnp.dot(stride_v[t], rows[t], preferred_element_type=jnp.float32)

        def join(m, y_hi, z, core, chunk=chunk):
            for x in range(4):
                r = pl.ds(pl.multiple_of(m * 32 + x * 8, 8), 8)
                top = paired(mixed[0, r, :], mixed[1, r, :])
                bottom = paired(mixed[2, r, :], mixed[3, r, :])
                for y_lo in range(2):
                    slot = send_slot(ORDERS[chunk], (x, y_hi * 2 + y_lo, z, core))
                    ret0[(chunk, *slot)] = jnp.concatenate([top[y_lo], bottom[y_lo]], axis=0).astype(jnp.bfloat16)

        each_octet(join)
        back[chunk].start(0)

    gather.wait(3)
    gather.start(4)
    for chunk in range(CHUNKS):
        back[chunk].wait(0)
        back[chunk].start(1)
    gather.wait(4)
    for k in range(3):

        def add_squares(i, sums, k=k):
            w = weights[k, pl.ds(pl.multiple_of(i * 64, 64), 64), :].astype(jnp.float32)
            return sums + jnp.sum((w * w).reshape(8, 8, 768), axis=0)

        sums = lax.fori_loop(0, 12, add_squares, jnp.zeros((8, 768), jnp.float32))
        squares = jnp.sum(sums, axis=0, keepdims=True)
        colscale[pl.ds(k, 1), :] = scales[pl.ds(k, 1), :] * lax.rsqrt(squares + 1e-06)
    out_scale[...] = colscale[pl.ds(2, 1), :]
    stores = [pltpu.make_async_copy(weights.at[2], out_proj, out_sems.at[4])]
    stores[0].start()

    def gate_block(i):
        r = pl.ds((i % 2) * 256, 256)
        gate = jnp.dot(normed[i // 2, r, :], weights[1], preferred_element_type=jnp.float32)
        gate = (gate * colscale[pl.ds(1, 1), :]).astype(jnp.bfloat16).astype(jnp.float32)
        gate = gate / (1.0 + jnp.exp(-gate)) * colscale[pl.ds(0, 1), :]
        normed[i // 2, r, :] = gate.astype(jnp.bfloat16)

    for chunk in range(CHUNKS):
        back[chunk].wait(1)
        back[chunk].start(2)
        for i in ((0, 1), (2, 3), (4,), (5,), (6,), (7,))[chunk]:
            gate_block(i)

    for chunk in range(CHUNKS):
        back[chunk].wait(2)

        def unpack(m, y_hi, z, core, chunk=chunk):
            for x in range(4):
                for y_lo in range(2):
                    r = pl.ds(pl.multiple_of((m * 8 + x * 2 + y_lo) * PIECE, PIECE), PIECE)
                    slot = landed_slot(ORDERS[chunk], (x, y_hi * 2 + y_lo, z, core))
                    wide[chunk % 2, r, :] = ret3[(chunk, *slot)].astype(jnp.float32)

        each_octet(unpack)
        for a in range(4):
            part = wide[chunk % 2, pl.ds(a, 512, stride=4), :].astype(jnp.bfloat16)
            carried[a, :, pl.ds(chunk % 2 * WIDTH, WIDTH)] = part
        if chunk % 2 == 0:
            continue
        right = weights.at[0, pl.ds((chunk - 1) * WIDTH, 2 * WIDTH), :]

        for a in range(4):
            part = jnp.dot(carried[a], right[...], preferred_element_type=jnp.float32)
            if chunk == 1:
                total[a] = part
            elif chunk < CHUNKS - 1:
                total[a] = total[a] + part
            else:
                part = (total[a] + part) * normed[a].astype(jnp.float32)
                normed[a] = part.astype(jnp.bfloat16)
                stores.append(pltpu.make_async_copy(normed.at[a], out.at[a], out_sems.at[a]))
                stores[-1].start()
    for chunk in range(CHUNKS):
        for hop in range(3):
            forward[chunk].wait_sent(hop, rows)
            back[chunk].wait_sent(hop, rows)
    for hop in range(5):
        gather.wait_sent(hop)
    for store in stores:
        store.wait()


def mix(tokens, gain, block_w, stride_w, proj_w, scales):
    sent = (CHUNKS, 4, 2, 4, 4, PIECE, WIDTH)
    half_way = (CHUNKS, 4, 4, 2, 4, PIECE, WIDTH)
    landed = (CHUNKS, 4, 4, 4, 2, PIECE, WIDTH)
    bf16, f32 = jnp.bfloat16, jnp.float32
    hbm, vmem = pl.BlockSpec(memory_space=pl.ANY), pl.BlockSpec(memory_space=pltpu.VMEM)
    return pl.pallas_call(
        mix_kernel,
        out_shape=[
            pltpu.VMEM((4, 512, 768), bf16),
            pltpu.VMEM((768, 768), bf16),
            pltpu.VMEM((1, 768), f32),
        ],
        in_specs=[hbm, vmem, hbm, hbm, hbm, vmem],
        out_specs=[hbm, hbm, vmem],
        scratch_shapes=[
            pltpu.VMEM((4, 512, 768), bf16),
            pltpu.VMEM((4, 512, 512), bf16),
            pltpu.VMEM((4, 512, 512), bf16),
            pltpu.VMEM((3, 768, 768), bf16),
            pltpu.VMEM((3, 768), f32),
            pltpu.VMEM((2, 2048, WIDTH), f32),
            pltpu.VMEM((4, 512, WIDTH), bf16),
            pltpu.VMEM((4, 512, WIDTH), f32),
            pltpu.VMEM((4, 512, 2 * WIDTH), bf16),
            pltpu.VMEM((4, 512, 768), f32),
            *[pltpu.VMEM(s, bf16) for s in (sent, sent, half_way, landed)],
            *[pltpu.VMEM(s, bf16) for s in (sent, sent, half_way, landed)],
            pltpu.SemaphoreType.DMA((7,)),
            pltpu.SemaphoreType.DMA((5,)),
            *[pltpu.SemaphoreType.DMA((6 * CHUNKS,)) for _ in range(2)],
            *[pltpu.SemaphoreType.DMA((5,)) for _ in range(2)],
        ],
        compiler_params=pltpu.CompilerParams(collective_id=0, has_side_effects=True, vmem_limit_bytes=52 << 20),
        name="monarch_mix",
    )(tokens, gain, block_w, stride_w, proj_w, scales)


def project_kernel(hidden, weight, scale, out, result, sems):
    stores = []
    for i in range(4):
        product = jnp.dot(hidden[i], weight[...], preferred_element_type=jnp.float32)
        result[i] = (product * scale[...]).astype(jnp.bfloat16)
        stores.append(pltpu.make_async_copy(result.at[i], out.at[i], sems.at[i]))
        stores[-1].start()
    for store in stores:
        store.wait()


def project_out(hidden, weight, scale):
    vmem = pl.BlockSpec(memory_space=pltpu.VMEM)
    return pl.pallas_call(
        project_kernel,
        out_shape=jax.ShapeDtypeStruct(hidden.shape, jnp.bfloat16),
        in_specs=[vmem, vmem, vmem],
        out_specs=pl.BlockSpec(memory_space=pl.ANY),
        scratch_shapes=[pltpu.VMEM(hidden.shape, jnp.bfloat16), pltpu.SemaphoreType.DMA((4,))],
        compiler_params=pltpu.CompilerParams(vmem_limit_bytes=24 << 20),
        name="project_out",
    )(
        pltpu.with_memory_space_constraint(hidden, pltpu.VMEM),
        pltpu.with_memory_space_constraint(weight, pltpu.VMEM),
        pltpu.with_memory_space_constraint(scale, pltpu.VMEM),
    )


def local(tokens, norm_gain, block_weights, stride_weights, proj_weights, proj_scales):
    channels = tokens.shape[-1]
    hidden, out_weight, out_scale = mix(
        tokens.reshape(4, 512, channels), norm_gain, block_weights, stride_weights, proj_weights, proj_scales
    )
    return project_out(hidden, out_weight, out_scale).reshape(tokens.shape)


def solution(mesh):
    placed = (
        P(None, ("ctx", "chan"), None),
        P(),
        P(("ctx", "chan"), None, None),
        P(("ctx", "chan"), None, None),
        P(None, "chan", None),
        P(),
    )
    return jax.shard_map(
        local, mesh=mesh, in_specs=placed, out_specs=P(None, ("ctx", "chan"), None), check_vma=False
    )
```

```python
import functools

import jax
import jax.numpy as jnp
from jax import lax
from jax.experimental import pallas as pl
from jax.experimental.pallas import tpu as pltpu
from jax.sharding import PartitionSpec as P

MESH = pl.DeviceIdType.MESH
ORDERS = ((0, 1, 2), (1, 2, 0), (2, 0, 1)) * 2
CHUNKS = len(ORDERS)
WIDTH = 128
PIECE = 16
INNER, OUTER = pl.ds(0, 2), pl.ds(2, 1)


def coordinates():
    c, h = lax.axis_index("ctx"), lax.axis_index("chan")
    return h // 2, (c // 8) * 2 + h % 2, (c // 2) % 4, c % 2


def device_at(x, y, z, k):
    return (y // 2) * 8 + z * 2 + k, x * 2 + y % 2


def neighbour(me, offset):
    x, y, z, k = [(m + o) % n for m, o, n in zip(me, offset, (4, 4, 4, 2))]
    return device_at(x, y, z, k)


def along(axis, step, core=0):
    offset = [0, 0, 0, core]
    offset[axis] = step
    return tuple(offset)


PARTNERS = [along(axis, step, core) for axis in range(3) for step in (1, 3, 2) for core in (0, 1)] + [(0, 0, 0, 1)]


def send_slot(order, point):
    a, b, c = order
    return point[a], point[3], point[b], point[c]


def landed_slot(order, point):
    a, b, c = order
    return point[c], point[b], point[a], point[3]


class Journey:
    def __init__(self, me, chunk, buffers, sems, first_sem):
        self.me, self.chunk, self.buffers, self.sems, self.first_sem = me, chunk, buffers, sems, first_sem

    def copies(self, hop):
        me, chunk = self.me, self.chunk
        axis = ORDERS[chunk][hop]
        source, target = self.buffers[hop], self.buffers[hop + 1]
        here = me[axis]
        send_sem, recv_sem = [s.at[self.first_sem + hop] for s in self.sems]
        local, remote = [], []
        for core in (0, 1) if hop == 0 else (0,):
            for step in (0, 1, 3, 2):
                there = (here + step) % 4
                if hop == 0:
                    src = source.at[chunk, there, (me[3] + core) % 2]
                    dst = target.at[chunk, here, me[3]]
                elif hop == 1:
                    src, dst = source.at[chunk, :, :, there], target.at[chunk, here]
                else:
                    src, dst = source.at[chunk, :, :, :, there], target.at[chunk, here]
                offset = along(axis, step, core)
                if offset == (0, 0, 0, 0):
                    local.append((src, dst, recv_sem))
                else:
                    remote.append((src, dst, send_sem, recv_sem, neighbour(me, offset)))
        return local, remote

    def start(self, hop):
        local, remote = self.copies(hop)
        for src, dst, send_sem, recv_sem, device in remote:
            pltpu.make_async_remote_copy(
                src_ref=src, dst_ref=dst, send_sem=send_sem, recv_sem=recv_sem, device_id=device, device_id_type=MESH
            ).start()
        for src, dst, sem in local:
            pltpu.make_async_copy(src, dst, sem).start()


    def wait(self, hop):
        whole = self.buffers[hop + 1].at[self.chunk]
        pltpu.make_async_copy(whole, whole, self.sems[1].at[self.first_sem + hop]).wait()

    def wait_sent(self, hop, rows):
        if hop == 0:
            sent = rows.at[:, pl.ds(0, 448), :]
        else:
            sent = self.buffers[hop].at[self.chunk, pl.ds(0, 3)]
        pltpu.make_async_copy(sent, sent, self.sems[0].at[self.first_sem + hop]).wait()


class Gather:
    def __init__(self, me, proj_w, weights, send_sems, recv_sems):
        self.me, self.proj_w, self.weights, self.send_sems, self.recv_sems = me, proj_w, weights, send_sems, recv_sems
        self.x, self.y_lo = me[0], me[1] % 2
        self.mine = self.x * 2 + self.y_lo
        self.columns = pl.ds(pl.multiple_of(me[3] * 384, 128), 384)

    def shard(self, h, first=0, rows=96):
        return self.weights.at[:, pl.ds(pl.multiple_of(h * 96 + first, PIECE), rows), :]

    def part(self, h, first, rows, which):
        return self.weights.at[which, pl.ds(pl.multiple_of(h * 96 + first, PIECE), rows), self.columns]

    def copies(self, hop):
        me, x = self.me, self.x
        half = (me[2] % 2) * 48
        if hop == 0:
            for first, step in ((0, 1), (48, 3)):
                yield self.proj_w.at[INNER, pl.ds(first, 48), self.columns], self.part(self.mine, first, 48, INNER), along(1, step)
        elif hop == 1:
            for step in (1, 3):
                for y_lo in range(2):
                    ref = self.part(x * 2 + y_lo, half, 48, INNER)
                    yield ref, ref, along(0, step)
                ref = self.part(self.mine, half, 48, OUTER)
                yield ref, ref, along(0, step)
        elif hop == 2:
            for y_lo, step in ((0, 1), (1, 3)):
                ref = self.part(((x + 4 - step) % 4) * 2 + y_lo, half, 48, INNER)
                yield ref, ref, along(0, step)
            step = 1 + 2 * me[3]
            ref = self.part(((x + 4 - step) % 4) * 2 + self.y_lo, half, 48, OUTER)
            yield ref, ref, along(0, step)
        elif hop == 3:
            for other in (1, 2, 3):
                for y_lo, step in ((0, 1), (1, 3)):
                    ref = self.part(((x + other) % 4) * 2 + y_lo, half, 48, INNER)
                    yield ref, ref, along(2, step)
                ref = self.part(((x + other) % 4) * 2 + self.y_lo, half, 48, OUTER)
                yield ref, ref, along(2, 1 + 2 * ((other + me[3]) % 2))
        elif hop == 4:
            for other, step in enumerate((1, 3, 1, 3)):
                ref = self.part(other * 2 + self.y_lo, 0, 96, OUTER)
                yield ref, ref, along(1, step)
            ref = self.part(x * 2 + 1 - self.y_lo, 0, 96, INNER)
            yield ref, ref, (0, 0, 0, 1)
            for other in (1, 2, 3):
                ref = self.part(((x + other) % 4) * 2, 0, 192, INNER)
                yield ref, ref, (0, 0, 0, 1)
        else:
            ref = self.part(x * 2 + 1 - self.y_lo, 0, 96, OUTER)
            yield ref, ref, (0, 0, 0, 1)
            for other in (1, 2, 3):
                ref = self.part(((x + other) % 4) * 2, 0, 192, OUTER)
                yield ref, ref, (0, 0, 0, 1)

    def start(self, hop):
        for src, dst, offset in self.copies(hop):
            pltpu.make_async_remote_copy(
                src_ref=src,
                dst_ref=dst,
                send_sem=self.send_sems.at[hop],
                recv_sem=self.recv_sems.at[hop],
                device_id=neighbour(self.me, offset),
                device_id_type=MESH,
            ).start()

    def _wait(self, sems, hop):
        ref = self.weights.at[:, pl.ds(0, (64, 160, 80, 240, 576, 224)[hop]), pl.ds(0, 384)]
        pltpu.make_async_copy(ref, ref, sems.at[hop]).wait()

    def wait(self, hop):
        self._wait(self.recv_sems, hop)

    def wait_sent(self, hop):
        self._wait(self.send_sems, hop)


def each_octet(body):
    def step(m, carry):
        body(m, m // 8, (m // 2) % 4, m % 2)
        return carry

    lax.fori_loop(0, 16, step, 0)


def mix_kernel(
    tokens,
    gain,
    block_w,
    stride_w,
    proj_w,
    scales,
    normed,
    out_proj,
    out_scale,
    block_v,
    stride_v,
    weights,
    colscale,
    wide,
    rows,
    mixed,
    carried,
    total,
    fwd0,
    fwd1,
    fwd2,
    fwd3,
    ret0,
    ret1,
    ret2,
    ret3,
    load_sems,
    out_sem,
    send_sems,
    recv_sems,
    gather_send,
    gather_recv,
):
    me = coordinates()
    sems = (send_sems, recv_sems)
    loads = [pltpu.make_async_copy(tokens.at[b], normed.at[b], load_sems.at[b]) for b in range(4)]
    loads.append(pltpu.make_async_copy(block_w, block_v, load_sems.at[4]))
    loads.append(pltpu.make_async_copy(stride_w, stride_v, load_sems.at[5]))
    gather = Gather(me, proj_w, weights, gather_send, gather_recv)
    loads.append(pltpu.make_async_copy(proj_w, gather.shard(gather.mine), load_sems.at[6]))
    for load in loads[:5]:
        load.start()
    barrier = pltpu.get_barrier_semaphore()
    for offset in PARTNERS:
        pl.semaphore_signal(barrier, inc=1, device_id=neighbour(me, offset), device_id_type=MESH)

    for b in range(4):
        loads[b].wait()

        def norm(i, carry, b=b):
            r = pl.ds(pl.multiple_of(i * 64, 64), 64)
            x = normed[b, r, :].astype(jnp.float32)
            scale = lax.rsqrt(jnp.mean(x * x, axis=-1, keepdims=True) + 1e-05)
            normed[b, r, :] = (x * scale * gain[...][None, :]).astype(jnp.bfloat16)
            return carry

        lax.fori_loop(0, 8, norm, 0)
    pl.semaphore_wait(barrier, len(PARTNERS))
    gather.start(0)
    loads[4].wait()
    for load in loads[5:]:
        load.start()

    forward = [Journey(me, c, (fwd0, fwd1, fwd2, fwd3), sems, 3 * c) for c in range(CHUNKS)]
    back = [Journey(me, c, (ret0, ret1, ret2, ret3), sems, 3 * (CHUNKS + c)) for c in range(CHUNKS)]

    low = lax.broadcasted_iota(jnp.int32, (8, WIDTH), 0) < 4

    def paired(p, q):
        return jnp.where(low, p, pltpu.roll(q, 4, 0)), jnp.where(low, pltpu.roll(p, 4, 0), q)

    for first, count in ((0, 2), (2, 1), (3, 1), (4, 2)):
        for b in range(4):
            columns = pl.ds(first * WIDTH, count * WIDTH)
            x = jnp.dot(block_v[b], normed[b, :, columns], preferred_element_type=jnp.float32)
            for half in range(count):
                wide[half, pl.ds(b, 512, stride=4), :] = x[:, half * WIDTH : (half + 1) * WIDTH]
        for half in range(count):
            chunk = first + half

            def pack(m, y_hi, z, core, half=half, chunk=chunk):
                for x in range(4):
                    for y_lo in range(2):
                        r = pl.ds(pl.multiple_of((m * 8 + x * 2 + y_lo) * PIECE, PIECE), PIECE)
                        slot = send_slot(ORDERS[chunk], (x, y_hi * 2 + y_lo, z, core))
                        fwd0[(chunk, *slot)] = wide[half, r, :].astype(jnp.bfloat16)

            each_octet(pack)
            forward[chunk].start(0)

    loads[6].wait()
    gather.wait(0)
    gather.start(1)
    for hop in range(2):
        for chunk in range(CHUNKS):
            forward[chunk].wait(hop)
            forward[chunk].start(hop + 1)
        gather.wait(hop + 1)
        gather.start(hop + 2)
    loads[5].wait()

    for chunk in range(CHUNKS):
        forward[chunk].wait(2)

        def split(m, y_hi, z, core, chunk=chunk):
            per_t = [[] for _ in range(4)]
            for x in range(4):
                even, odd = [
                    fwd3[(chunk, *landed_slot(ORDERS[chunk], (x, y_hi * 2 + y_lo, z, core)))].astype(jnp.float32)
                    for y_lo in range(2)
                ]
                for j in range(2):
                    first, second = paired(even[8 * j : 8 * j + 8], odd[8 * j : 8 * j + 8])
                    per_t[2 * j].append(first)
                    per_t[2 * j + 1].append(second)
            r = pl.ds(pl.multiple_of(m * 32, 32), 32)
            for t in range(4):
                rows[t, r, :] = jnp.concatenate(per_t[t], axis=0).astype(jnp.bfloat16)

        each_octet(split)
        for t in range(4):
            mixed[t] = jnp.dot(stride_v[t], rows[t], preferred_element_type=jnp.float32)

        def join(m, y_hi, z, core, chunk=chunk):
            for x in range(4):
                r = pl.ds(pl.multiple_of(m * 32 + x * 8, 8), 8)
                top = paired(mixed[0, r, :], mixed[1, r, :])
                bottom = paired(mixed[2, r, :], mixed[3, r, :])
                for y_lo in range(2):
                    slot = send_slot(ORDERS[chunk], (x, y_hi * 2 + y_lo, z, core))
                    ret0[(chunk, *slot)] = jnp.concatenate([top[y_lo], bottom[y_lo]], axis=0).astype(jnp.bfloat16)

        each_octet(join)
        back[chunk].start(0)

    gather.wait(3)
    gather.start(4)
    for chunk in range(CHUNKS):
        back[chunk].wait(0)
        back[chunk].start(1)
    gather.wait(4)
    gather.start(5)

    def scale_columns(k):
        def add_squares(i, sums):
            w = weights[k, pl.ds(pl.multiple_of(i * 64, 64), 64), :].astype(jnp.float32)
            return sums + jnp.sum((w * w).reshape(8, 8, 768), axis=0)

        sums = lax.fori_loop(0, 12, add_squares, jnp.zeros((8, 768), jnp.float32))
        squares = jnp.sum(sums, axis=0, keepdims=True)
        colscale[pl.ds(k, 1), :] = scales[pl.ds(k, 1), :] * lax.rsqrt(squares + 1e-06)

    scale_columns(0)
    scale_columns(1)

    def gate_block(i):
        r = pl.ds((i % 2) * 256, 256)
        gate = jnp.dot(normed[i // 2, r, :], weights[1], preferred_element_type=jnp.float32)
        gate = (gate * colscale[pl.ds(1, 1), :]).astype(jnp.bfloat16).astype(jnp.float32)
        gate = gate / (1.0 + jnp.exp(-gate)) * colscale[pl.ds(0, 1), :]
        normed[i // 2, r, :] = gate.astype(jnp.bfloat16)

    for i in range(8):
        gate_block(i)
    for chunk in range(CHUNKS):
        back[chunk].wait(1)
        back[chunk].start(2)
    gather.wait(5)
    scale_columns(2)
    out_scale[...] = colscale[pl.ds(2, 1), :]
    store = pltpu.make_async_copy(weights.at[2], out_proj, out_sem)
    store.start()

    for chunk in range(CHUNKS):
        back[chunk].wait(2)

        def unpack(m, y_hi, z, core, chunk=chunk):
            for x in range(4):
                for y_lo in range(2):
                    r = pl.ds(pl.multiple_of((m * 8 + x * 2 + y_lo) * PIECE, PIECE), PIECE)
                    slot = landed_slot(ORDERS[chunk], (x, y_hi * 2 + y_lo, z, core))
                    wide[chunk % 2, r, :] = ret3[(chunk, *slot)].astype(jnp.float32)

        each_octet(unpack)
        for a in range(4):
            part = wide[chunk % 2, pl.ds(a, 512, stride=4), :].astype(jnp.bfloat16)
            carried[a, :, pl.ds(chunk % 2 * WIDTH, WIDTH)] = part
        if chunk % 2 == 0:
            continue
        right = weights.at[0, pl.ds((chunk - 1) * WIDTH, 2 * WIDTH), :]

        for a in range(4):
            part = jnp.dot(carried[a], right[...], preferred_element_type=jnp.float32)
            if chunk == 1:
                total[a] = part
            elif chunk < CHUNKS - 1:
                total[a] = total[a] + part
            else:
                part = (total[a] + part) * normed[a].astype(jnp.float32)
                normed[a] = part.astype(jnp.bfloat16)
    for chunk in range(CHUNKS):
        for hop in range(3):
            forward[chunk].wait_sent(hop, rows)
            back[chunk].wait_sent(hop, rows)
    for hop in range(6):
        gather.wait_sent(hop)
    store.wait()


def mix(tokens, gain, block_w, stride_w, proj_w, scales):
    sent = (CHUNKS, 4, 2, 4, 4, PIECE, WIDTH)
    half_way = (CHUNKS, 4, 4, 2, 4, PIECE, WIDTH)
    landed = (CHUNKS, 4, 4, 4, 2, PIECE, WIDTH)
    bf16, f32 = jnp.bfloat16, jnp.float32
    hbm, vmem = pl.BlockSpec(memory_space=pl.ANY), pl.BlockSpec(memory_space=pltpu.VMEM)
    return pl.pallas_call(
        mix_kernel,
        out_shape=[
            pltpu.VMEM((4, 512, 768), bf16),
            pltpu.VMEM((768, 768), bf16),
            pltpu.VMEM((1, 768), f32),
        ],
        in_specs=[hbm, vmem, hbm, hbm, hbm, vmem],
        out_specs=[vmem, hbm, vmem],
        scratch_shapes=[
            pltpu.VMEM((4, 512, 512), bf16),
            pltpu.VMEM((4, 512, 512), bf16),
            pltpu.VMEM((3, 768, 768), bf16),
            pltpu.VMEM((3, 768), f32),
            pltpu.VMEM((2, 2048, WIDTH), f32),
            pltpu.VMEM((4, 512, WIDTH), bf16),
            pltpu.VMEM((4, 512, WIDTH), f32),
            pltpu.VMEM((4, 512, 2 * WIDTH), bf16),
            pltpu.VMEM((4, 512, 768), f32),
            *[pltpu.VMEM(s, bf16) for s in (sent, sent, half_way, landed)],
            *[pltpu.VMEM(s, bf16) for s in (sent, sent, half_way, landed)],
            pltpu.SemaphoreType.DMA((7,)),
            pltpu.SemaphoreType.DMA,
            *[pltpu.SemaphoreType.DMA((6 * CHUNKS,)) for _ in range(2)],
            *[pltpu.SemaphoreType.DMA((6,)) for _ in range(2)],
        ],
        compiler_params=pltpu.CompilerParams(collective_id=0, has_side_effects=True, vmem_limit_bytes=52 << 20),
        name="monarch_mix",
    )(tokens, gain, block_w, stride_w, proj_w, scales)


def project_kernel(hidden, weight, scale, out, result, sems):
    stores = []
    for i in range(4):
        product = jnp.dot(hidden[i], weight[...], preferred_element_type=jnp.float32)
        result[i] = (product * scale[...]).astype(jnp.bfloat16)
        stores.append(pltpu.make_async_copy(result.at[i], out.at[i], sems.at[i]))
        stores[-1].start()
    for store in stores:
        store.wait()


def project_out(hidden, weight, scale):
    vmem = pl.BlockSpec(memory_space=pltpu.VMEM)
    return pl.pallas_call(
        project_kernel,
        out_shape=jax.ShapeDtypeStruct(hidden.shape, jnp.bfloat16),
        in_specs=[vmem, vmem, vmem],
        out_specs=pl.BlockSpec(memory_space=pl.ANY),
        scratch_shapes=[pltpu.VMEM(hidden.shape, jnp.bfloat16), pltpu.SemaphoreType.DMA((4,))],
        compiler_params=pltpu.CompilerParams(vmem_limit_bytes=24 << 20),
        name="project_out",
    )(
        pltpu.with_memory_space_constraint(hidden, pltpu.VMEM),
        pltpu.with_memory_space_constraint(weight, pltpu.VMEM),
        pltpu.with_memory_space_constraint(scale, pltpu.VMEM),
    )


def local(tokens, norm_gain, block_weights, stride_weights, proj_weights, proj_scales):
    channels = tokens.shape[-1]
    hidden, out_weight, out_scale = mix(
        tokens.reshape(4, 512, channels), norm_gain, block_weights, stride_weights, proj_weights, proj_scales
    )
    return project_out(hidden, out_weight, out_scale).reshape(tokens.shape)


def solution(mesh):
    placed = (
        P(None, ("ctx", "chan"), None),
        P(),
        P(("ctx", "chan"), None, None),
        P(("ctx", "chan"), None, None),
        P(None, "chan", None),
        P(),
    )
    return jax.shard_map(
        local, mesh=mesh, in_specs=placed, out_specs=P(None, ("ctx", "chan"), None), check_vma=False
    )
```

```python
import functools

import jax
import jax.numpy as jnp
from jax import lax
from jax.experimental import pallas as pl
from jax.experimental.pallas import tpu as pltpu
from jax.sharding import PartitionSpec as P

MESH = pl.DeviceIdType.MESH
ORDERS = ((0, 1, 2), (1, 2, 0), (2, 0, 1)) * 2
CHUNKS = len(ORDERS)
WIDTH = 128
PIECE = 16
GROUPS = ((0, 1, 2), (3, 4, 5))
INNER, OUTER = pl.ds(0, 2), pl.ds(2, 1)


def coordinates():
    c, h = lax.axis_index("ctx"), lax.axis_index("chan")
    return h // 2, (c // 8) * 2 + h % 2, (c // 2) % 4, c % 2


def device_at(x, y, z, k):
    return (y // 2) * 8 + z * 2 + k, x * 2 + y % 2


def neighbour(me, offset):
    x, y, z, k = [(m + o) % n for m, o, n in zip(me, offset, (4, 4, 4, 2))]
    return device_at(x, y, z, k)


def along(axis, step, core=0):
    offset = [0, 0, 0, core]
    offset[axis] = step
    return tuple(offset)


PARTNERS = [along(axis, step, core) for axis in range(3) for step in (1, 3, 2) for core in (0, 1)] + [(0, 0, 0, 1)]


def send_slot(order, point):
    a, b, c = order
    return point[a], point[3], point[b], point[c]


def landed_slot(order, point):
    a, b, c = order
    return point[c], point[b], point[a], point[3]


class Journey:
    def __init__(self, me, chunk, buffers, sems, first_sem):
        self.me, self.chunk, self.buffers, self.sems, self.first_sem = me, chunk, buffers, sems, first_sem

    def copies(self, hop):
        me, chunk = self.me, self.chunk
        axis = ORDERS[chunk][hop]
        source, target = self.buffers[hop], self.buffers[hop + 1]
        here = me[axis]
        send_sem, recv_sem = [s.at[self.first_sem + hop] for s in self.sems]
        local, remote = [], []
        for core in (0, 1) if hop == 0 else (0,):
            for step in (0, 1, 3, 2):
                there = (here + step) % 4
                if hop == 0:
                    src = source.at[chunk, there, (me[3] + core) % 2]
                    dst = target.at[chunk, here, me[3]]
                elif hop == 1:
                    src, dst = source.at[chunk, :, :, there], target.at[chunk, here]
                else:
                    src, dst = source.at[chunk, :, :, :, there], target.at[chunk, here]
                offset = along(axis, step, core)
                if offset == (0, 0, 0, 0):
                    local.append((src, dst, recv_sem))
                else:
                    remote.append((src, dst, send_sem, recv_sem, neighbour(me, offset)))
        return local, remote

    def start(self, hop):
        local, remote = self.copies(hop)
        for src, dst, send_sem, recv_sem, device in remote:
            pltpu.make_async_remote_copy(
                src_ref=src, dst_ref=dst, send_sem=send_sem, recv_sem=recv_sem, device_id=device, device_id_type=MESH
            ).start()
        for src, dst, sem in local:
            pltpu.make_async_copy(src, dst, sem).start()


    def wait(self, hop):
        whole = self.buffers[hop + 1].at[self.chunk]
        pltpu.make_async_copy(whole, whole, self.sems[1].at[self.first_sem + hop]).wait()

    def wait_sent(self, hop, rows):
        if hop == 0:
            sent = rows.at[:, pl.ds(0, 448), :]
        else:
            sent = self.buffers[hop].at[self.chunk, pl.ds(0, 3)]
        pltpu.make_async_copy(sent, sent, self.sems[0].at[self.first_sem + hop]).wait()


class Gather:
    def __init__(self, me, proj_w, weights, send_sems, recv_sems):
        self.me, self.proj_w, self.weights, self.send_sems, self.recv_sems = me, proj_w, weights, send_sems, recv_sems
        self.x, self.y_lo = me[0], me[1] % 2
        self.mine = self.x * 2 + self.y_lo
        self.columns = pl.ds(pl.multiple_of(me[3] * 384, 128), 384)

    def shard(self, h, first=0, rows=96):
        return self.weights.at[:, pl.ds(pl.multiple_of(h * 96 + first, PIECE), rows), :]

    def part(self, h, first, rows, which):
        return self.weights.at[which, pl.ds(pl.multiple_of(h * 96 + first, PIECE), rows), self.columns]

    def copies(self, hop):
        me, x = self.me, self.x
        half = (me[2] % 2) * 48
        if hop == 0:
            for first, step in ((0, 1), (48, 3)):
                yield self.proj_w.at[INNER, pl.ds(first, 48), self.columns], self.part(self.mine, first, 48, INNER), along(1, step)
            mine = pl.ds(pl.multiple_of(half, PIECE), 48)
            for step in (1, 3):
                yield self.proj_w.at[:, mine, self.columns], self.part(self.mine, half, 48, slice(None)), along(0, step)
        elif hop == 1:
            for step in (1, 3):
                ref = self.part(x * 2 + 1 - self.y_lo, half, 48, INNER)
                yield ref, ref, along(0, step)
        elif hop == 2:
            for y_lo, step in ((0, 1), (1, 3)):
                ref = self.part(((x + 4 - step) % 4) * 2 + y_lo, half, 48, INNER)
                yield ref, ref, along(0, step)
            step = 1 + 2 * me[3]
            ref = self.part(((x + 4 - step) % 4) * 2 + self.y_lo, half, 48, OUTER)
            yield ref, ref, along(0, step)
        elif hop == 3:
            for other in (1, 2, 3):
                for y_lo, step in ((0, 1), (1, 3)):
                    ref = self.part(((x + other) % 4) * 2 + y_lo, half, 48, INNER)
                    yield ref, ref, along(2, step)
                ref = self.part(((x + other) % 4) * 2 + self.y_lo, half, 48, OUTER)
                yield ref, ref, along(2, 1 + 2 * ((other + me[3]) % 2))
        elif hop == 4:
            for other, step in enumerate((1, 3, 1, 3)):
                ref = self.part(other * 2 + self.y_lo, 0, 96, OUTER)
                yield ref, ref, along(1, step)
            ref = self.part(x * 2 + 1 - self.y_lo, 0, 96, INNER)
            yield ref, ref, (0, 0, 0, 1)
            for other in (1, 2, 3):
                ref = self.part(((x + other) % 4) * 2, 0, 192, INNER)
                yield ref, ref, (0, 0, 0, 1)
        else:
            ref = self.part(x * 2 + 1 - self.y_lo, 0, 96, OUTER)
            yield ref, ref, (0, 0, 0, 1)
            for other in (1, 2, 3):
                ref = self.part(((x + other) % 4) * 2, 0, 192, OUTER)
                yield ref, ref, (0, 0, 0, 1)

    def start(self, hop):
        for src, dst, offset in self.copies(hop):
            pltpu.make_async_remote_copy(
                src_ref=src,
                dst_ref=dst,
                send_sem=self.send_sems.at[hop],
                recv_sem=self.recv_sems.at[hop],
                device_id=neighbour(self.me, offset),
                device_id_type=MESH,
            ).start()

    def _wait(self, sems, hop):
        ref = self.weights.at[:, pl.ds(0, (160, 64, 80, 240, 576, 224)[hop]), pl.ds(0, 384)]
        pltpu.make_async_copy(ref, ref, sems.at[hop]).wait()

    def wait(self, hop):
        self._wait(self.recv_sems, hop)

    def wait_sent(self, hop):
        self._wait(self.send_sems, hop)


def each_octet(body):
    def step(m, carry):
        body(m, m // 8, (m // 2) % 4, m % 2)
        return carry

    lax.fori_loop(0, 16, step, 0)


def mix_kernel(
    tokens,
    gain,
    block_w,
    stride_w,
    proj_w,
    scales,
    normed,
    out_proj,
    out_scale,
    block_v,
    stride_v,
    weights,
    colscale,
    wide,
    rows,
    mixed,
    carried,
    total,
    fwd0,
    fwd1,
    fwd2,
    fwd3,
    ret0,
    ret1,
    ret2,
    ret3,
    load_sems,
    out_sem,
    send_sems,
    recv_sems,
    gather_send,
    gather_recv,
):
    me = coordinates()
    sems = (send_sems, recv_sems)
    loads = [pltpu.make_async_copy(tokens.at[b], normed.at[b], load_sems.at[b]) for b in range(4)]
    loads.append(pltpu.make_async_copy(block_w, block_v, load_sems.at[4]))
    loads.append(pltpu.make_async_copy(stride_w, stride_v, load_sems.at[5]))
    gather = Gather(me, proj_w, weights, gather_send, gather_recv)
    loads.append(pltpu.make_async_copy(proj_w, gather.shard(gather.mine), load_sems.at[6]))
    for load in loads[:4]:
        load.start()
    barrier = pltpu.get_barrier_semaphore()
    for offset in PARTNERS:
        pl.semaphore_signal(barrier, inc=1, device_id=neighbour(me, offset), device_id_type=MESH)

    loads[4].start()

    for b in range(4):
        loads[b].wait()

        def norm(i, carry, b=b):
            r = pl.ds(pl.multiple_of(i * 128, 128), 128)
            tiles = [pl.ds(n * WIDTH, WIDTH) for n in range(CHUNKS)]
            squares = jnp.zeros((128, WIDTH), jnp.float32)
            for c in tiles:
                x = normed[b, r, c].astype(jnp.float32)
                squares = squares + x * x
            scale = lax.rsqrt(jnp.sum(squares, axis=-1, keepdims=True) / 768 + 1e-05)
            for c in tiles:
                x = normed[b, r, c].astype(jnp.float32)
                normed[b, r, c] = (x * scale * gain[c][None, :]).astype(jnp.bfloat16)
            return carry

        lax.fori_loop(0, 4, norm, 0)
    pl.semaphore_wait(barrier, len(PARTNERS))
    gather.start(0)
    loads[4].wait()
    for load in loads[5:]:
        load.start()

    forward = [Journey(me, c, (fwd0, fwd1, fwd2, fwd3), sems, 3 * c) for c in range(CHUNKS)]
    back = [Journey(me, c, (ret0, ret1, ret2, ret3), sems, 3 * (CHUNKS + c)) for c in range(CHUNKS)]

    low = lax.broadcasted_iota(jnp.int32, (8, WIDTH), 0) < 4

    def paired(p, q):
        return jnp.where(low, p, pltpu.roll(q, 4, 0)), jnp.where(low, pltpu.roll(p, 4, 0), q)

    for first, count in ((0, 2), (2, 2), (4, 2)):
        for b in range(4):
            columns = pl.ds(first * WIDTH, count * WIDTH)
            x = jnp.dot(block_v[b], normed[b, :, columns], preferred_element_type=jnp.float32)
            for half in range(count):
                wide[half, pl.ds(b, 512, stride=4), :] = x[:, half * WIDTH : (half + 1) * WIDTH]
        for half in range(count):
            chunk = first + half

            def pack(m, y_hi, z, core, half=half, chunk=chunk):
                for x in range(4):
                    for y_lo in range(2):
                        r = pl.ds(pl.multiple_of((m * 8 + x * 2 + y_lo) * PIECE, PIECE), PIECE)
                        slot = send_slot(ORDERS[chunk], (x, y_hi * 2 + y_lo, z, core))
                        fwd0[(chunk, *slot)] = wide[half, r, :].astype(jnp.bfloat16)

            each_octet(pack)
            forward[chunk].start(0)

    loads[6].wait()
    gather.wait(0)
    gather.start(1)
    for hop in range(2):
        for chunk in range(CHUNKS):
            forward[chunk].wait(hop)
            forward[chunk].start(hop + 1)
        gather.wait(hop + 1)
        gather.start(hop + 2)
    loads[5].wait()

    for chunk in range(CHUNKS):
        forward[chunk].wait(2)

        def split(m, y_hi, z, core, chunk=chunk):
            per_t = [[] for _ in range(4)]
            for x in range(4):
                even, odd = [
                    fwd3[(chunk, *landed_slot(ORDERS[chunk], (x, y_hi * 2 + y_lo, z, core)))].astype(jnp.float32)
                    for y_lo in range(2)
                ]
                for j in range(2):
                    first, second = paired(even[8 * j : 8 * j + 8], odd[8 * j : 8 * j + 8])
                    per_t[2 * j].append(first)
                    per_t[2 * j + 1].append(second)
            r = pl.ds(pl.multiple_of(m * 32, 32), 32)
            for t in range(4):
                rows[t, r, :] = jnp.concatenate(per_t[t], axis=0).astype(jnp.bfloat16)

        each_octet(split)
        for t in range(4):
            mixed[t] = jnp.dot(stride_v[t], rows[t], preferred_element_type=jnp.float32)

        def join(m, y_hi, z, core, chunk=chunk):
            for x in range(4):
                r = pl.ds(pl.multiple_of(m * 32 + x * 8, 8), 8)
                top = paired(mixed[0, r, :], mixed[1, r, :])
                bottom = paired(mixed[2, r, :], mixed[3, r, :])
                for y_lo in range(2):
                    slot = send_slot(ORDERS[chunk], (x, y_hi * 2 + y_lo, z, core))
                    ret0[(chunk, *slot)] = jnp.concatenate([top[y_lo], bottom[y_lo]], axis=0).astype(jnp.bfloat16)

        each_octet(join)
        back[chunk].start(0)

    gather.wait(3)
    gather.start(4)
    for chunk in range(CHUNKS):
        back[chunk].wait(0)
        back[chunk].start(1)
    gather.wait(4)
    gather.start(5)

    def scale_columns(k):
        def add_squares(i, sums):
            w = weights[k, pl.ds(pl.multiple_of(i * 64, 64), 64), :].astype(jnp.float32)
            return sums + jnp.sum((w * w).reshape(8, 8, 768), axis=0)

        sums = lax.fori_loop(0, 12, add_squares, jnp.zeros((8, 768), jnp.float32))
        squares = jnp.sum(sums, axis=0, keepdims=True)
        colscale[pl.ds(k, 1), :] = scales[pl.ds(k, 1), :] * lax.rsqrt(squares + 1e-06)

    scale_columns(0)
    scale_columns(1)

    def gate_block(i):
        r = pl.ds((i % 2) * 256, 256)
        gate = jnp.dot(normed[i // 2, r, :], weights[1], preferred_element_type=jnp.float32)
        gate = (gate * colscale[pl.ds(1, 1), :]).astype(jnp.bfloat16).astype(jnp.float32)
        gate = gate / (1.0 + jnp.exp(-gate)) * colscale[pl.ds(0, 1), :]
        normed[i // 2, r, :] = gate.astype(jnp.bfloat16)

    for i in range(8):
        gate_block(i)
    for chunk in range(CHUNKS):
        back[chunk].wait(1)
        back[chunk].start(2)
    gather.wait(5)
    scale_columns(2)
    out_scale[...] = colscale[pl.ds(2, 1), :]
    store = pltpu.make_async_copy(weights.at[2], out_proj, out_sem)
    store.start()

    for chunk in range(CHUNKS):
        back[chunk].wait(2)

        def unpack(m, y_hi, z, core, chunk=chunk):
            for x in range(4):
                for y_lo in range(2):
                    r = pl.ds(pl.multiple_of((m * 8 + x * 2 + y_lo) * PIECE, PIECE), PIECE)
                    slot = landed_slot(ORDERS[chunk], (x, y_hi * 2 + y_lo, z, core))
                    wide[chunk % 2, r, :] = ret3[(chunk, *slot)].astype(jnp.float32)

        each_octet(unpack)
        group = [g for g in GROUPS if chunk in g][0]
        place = pl.ds((chunk - group[0]) * WIDTH, WIDTH)
        for a in range(4):
            carried[a, :, place] = wide[chunk % 2, pl.ds(a, 512, stride=4), :].astype(jnp.bfloat16)
        if chunk != group[-1]:
            continue
        left, right = pl.ds(0, len(group) * WIDTH), pl.ds(group[0] * WIDTH, len(group) * WIDTH)
        for a in range(4):
            part = jnp.dot(carried[a, :, left], weights[0, right, :], preferred_element_type=jnp.float32)
            if group != GROUPS[0]:
                part = total[a] + part
            if group == GROUPS[-1]:
                normed[a] = (part * normed[a].astype(jnp.float32)).astype(jnp.bfloat16)
            else:
                total[a] = part
    for chunk in range(CHUNKS):
        for hop in range(3):
            forward[chunk].wait_sent(hop, rows)
            back[chunk].wait_sent(hop, rows)
    for hop in range(6):
        gather.wait_sent(hop)
    store.wait()


def mix(tokens, gain, block_w, stride_w, proj_w, scales):
    sent = (CHUNKS, 4, 2, 4, 4, PIECE, WIDTH)
    half_way = (CHUNKS, 4, 4, 2, 4, PIECE, WIDTH)
    landed = (CHUNKS, 4, 4, 4, 2, PIECE, WIDTH)
    bf16, f32 = jnp.bfloat16, jnp.float32
    hbm, vmem = pl.BlockSpec(memory_space=pl.ANY), pl.BlockSpec(memory_space=pltpu.VMEM)
    return pl.pallas_call(
        mix_kernel,
        out_shape=[
            pltpu.VMEM((4, 512, 768), bf16),
            pltpu.VMEM((768, 768), bf16),
            pltpu.VMEM((1, 768), f32),
        ],
        in_specs=[hbm, vmem, hbm, hbm, hbm, vmem],
        out_specs=[vmem, hbm, vmem],
        scratch_shapes=[
            pltpu.VMEM((4, 512, 512), bf16),
            pltpu.VMEM((4, 512, 512), bf16),
            pltpu.VMEM((3, 768, 768), bf16),
            pltpu.VMEM((3, 768), f32),
            pltpu.VMEM((2, 2048, WIDTH), f32),
            pltpu.VMEM((4, 512, WIDTH), bf16),
            pltpu.VMEM((4, 512, WIDTH), f32),
            pltpu.VMEM((4, 512, 3 * WIDTH), bf16),
            pltpu.VMEM((4, 512, 768), f32),
            *[pltpu.VMEM(s, bf16) for s in (sent, sent, half_way, landed)],
            *[pltpu.VMEM(s, bf16) for s in (sent, sent, half_way, landed)],
            pltpu.SemaphoreType.DMA((7,)),
            pltpu.SemaphoreType.DMA,
            *[pltpu.SemaphoreType.DMA((6 * CHUNKS,)) for _ in range(2)],
            *[pltpu.SemaphoreType.DMA((6,)) for _ in range(2)],
        ],
        compiler_params=pltpu.CompilerParams(collective_id=0, has_side_effects=True, vmem_limit_bytes=52 << 20),
        name="monarch_mix",
    )(tokens, gain, block_w, stride_w, proj_w, scales)


def project_kernel(hidden, weight, scale, out, result, sems):
    stores = []
    for i in range(4):
        product = jnp.dot(hidden[i], weight[...], preferred_element_type=jnp.float32)
        result[i] = (product * scale[...]).astype(jnp.bfloat16)
        stores.append(pltpu.make_async_copy(result.at[i], out.at[i], sems.at[i]))
        stores[-1].start()
    for store in stores:
        store.wait()


def project_out(hidden, weight, scale):
    vmem = pl.BlockSpec(memory_space=pltpu.VMEM)
    return pl.pallas_call(
        project_kernel,
        out_shape=jax.ShapeDtypeStruct(hidden.shape, jnp.bfloat16),
        in_specs=[vmem, vmem, vmem],
        out_specs=pl.BlockSpec(memory_space=pl.ANY),
        scratch_shapes=[pltpu.VMEM(hidden.shape, jnp.bfloat16), pltpu.SemaphoreType.DMA((4,))],
        compiler_params=pltpu.CompilerParams(vmem_limit_bytes=24 << 20),
        name="project_out",
    )(
        pltpu.with_memory_space_constraint(hidden, pltpu.VMEM),
        pltpu.with_memory_space_constraint(weight, pltpu.VMEM),
        pltpu.with_memory_space_constraint(scale, pltpu.VMEM),
    )


def local(tokens, norm_gain, block_weights, stride_weights, proj_weights, proj_scales):
    channels = tokens.shape[-1]
    hidden, out_weight, out_scale = mix(
        tokens.reshape(4, 512, channels), norm_gain, block_weights, stride_weights, proj_weights, proj_scales
    )
    return project_out(hidden, out_weight, out_scale).reshape(tokens.shape)


def solution(mesh):
    placed = (
        P(None, ("ctx", "chan"), None),
        P(),
        P(("ctx", "chan"), None, None),
        P(("ctx", "chan"), None, None),
        P(None, "chan", None),
        P(),
    )
    return jax.shard_map(
        local, mesh=mesh, in_specs=placed, out_specs=P(None, ("ctx", "chan"), None), check_vma=False
    )
```

```python
import functools

import jax
import jax.numpy as jnp
from jax import lax
from jax.experimental import pallas as pl
from jax.experimental.pallas import tpu as pltpu
from jax.sharding import PartitionSpec as P

MESH = pl.DeviceIdType.MESH
ORDERS = ((0, 1, 2), (1, 2, 0), (2, 0, 1)) * 2
CHUNKS = len(ORDERS)
WIDTH = 128
PIECE = 16
GROUPS = ((0, 1, 2), (3, 4, 5))
INNER, OUTER = pl.ds(0, 2), pl.ds(2, 1)


def coordinates():
    c, h = lax.axis_index("ctx"), lax.axis_index("chan")
    return h // 2, (c // 8) * 2 + h % 2, (c // 2) % 4, c % 2


def device_at(x, y, z, k):
    return (y // 2) * 8 + z * 2 + k, x * 2 + y % 2


def neighbour(me, offset):
    x, y, z, k = [(m + o) % n for m, o, n in zip(me, offset, (4, 4, 4, 2))]
    return device_at(x, y, z, k)


def along(axis, step, core=0):
    offset = [0, 0, 0, core]
    offset[axis] = step
    return tuple(offset)


PARTNERS = [along(axis, step, core) for axis in range(3) for step in (1, 3, 2) for core in (0, 1)] + [(0, 0, 0, 1)]


def send_slot(order, point):
    a, b, c = order
    return point[a], point[3], point[b], point[c]


def landed_slot(order, point):
    a, b, c = order
    return point[c], point[b], point[a], point[3]


class Journey:
    def __init__(self, me, chunk, buffers, sems, first_sem):
        self.me, self.chunk, self.buffers, self.sems, self.first_sem = me, chunk, buffers, sems, first_sem

    def copies(self, hop):
        me, chunk = self.me, self.chunk
        axis = ORDERS[chunk][hop]
        source, target = self.buffers[hop], self.buffers[hop + 1]
        here = me[axis]
        send_sem, recv_sem = [s.at[self.first_sem + hop] for s in self.sems]
        local, remote = [], []
        for core in (0, 1) if hop == 0 else (0,):
            for step in (0, 1, 3, 2):
                there = (here + step) % 4
                if hop == 0:
                    src = source.at[chunk, there, (me[3] + core) % 2]
                    dst = target.at[chunk, here, me[3]]
                elif hop == 1:
                    src, dst = source.at[chunk, :, :, there], target.at[chunk, here]
                else:
                    src, dst = source.at[chunk, :, :, :, there], target.at[chunk, here]
                offset = along(axis, step, core)
                if offset == (0, 0, 0, 0):
                    local.append((src, dst, recv_sem))
                else:
                    remote.append((src, dst, send_sem, recv_sem, neighbour(me, offset)))
        return local, remote

    def start(self, hop):
        local, remote = self.copies(hop)
        for src, dst, send_sem, recv_sem, device in remote:
            pltpu.make_async_remote_copy(
                src_ref=src, dst_ref=dst, send_sem=send_sem, recv_sem=recv_sem, device_id=device, device_id_type=MESH
            ).start()
        for src, dst, sem in local:
            pltpu.make_async_copy(src, dst, sem).start()


    def wait(self, hop):
        whole = self.buffers[hop + 1].at[self.chunk]
        pltpu.make_async_copy(whole, whole, self.sems[1].at[self.first_sem + hop]).wait()

    def wait_sent(self, hop, rows):
        if hop == 0:
            sent = rows.at[:, pl.ds(0, 448), :]
        else:
            sent = self.buffers[hop].at[self.chunk, pl.ds(0, 3)]
        pltpu.make_async_copy(sent, sent, self.sems[0].at[self.first_sem + hop]).wait()


class Gather:
    def __init__(self, me, proj_w, weights, send_sems, recv_sems):
        self.me, self.proj_w, self.weights, self.send_sems, self.recv_sems = me, proj_w, weights, send_sems, recv_sems
        self.x, self.y_lo = me[0], me[1] % 2
        self.mine = self.x * 2 + self.y_lo
        self.columns = pl.ds(pl.multiple_of(me[3] * 384, 128), 384)

    def shard(self, h, first=0, rows=96):
        return self.weights.at[:, pl.ds(pl.multiple_of(h * 96 + first, PIECE), rows), :]

    def part(self, h, first, rows, which):
        return self.weights.at[which, pl.ds(pl.multiple_of(h * 96 + first, PIECE), rows), self.columns]

    def copies(self, hop):
        me, x = self.me, self.x
        half = (me[2] % 2) * 48
        if hop == 0:
            for first, step in ((0, 1), (48, 3)):
                yield self.proj_w.at[INNER, pl.ds(first, 48), self.columns], self.part(self.mine, first, 48, INNER), along(1, step)
            mine = pl.ds(pl.multiple_of(half, PIECE), 48)
            for step in (1, 3):
                yield self.proj_w.at[:, mine, self.columns], self.part(self.mine, half, 48, slice(None)), along(0, step)
        elif hop == 1:
            for step in (1, 3):
                ref = self.part(x * 2 + 1 - self.y_lo, half, 48, INNER)
                yield ref, ref, along(0, step)
        elif hop == 2:
            for y_lo, step in ((0, 1), (1, 3)):
                ref = self.part(((x + 4 - step) % 4) * 2 + y_lo, half, 48, INNER)
                yield ref, ref, along(0, step)
            step = 1 + 2 * me[3]
            ref = self.part(((x + 4 - step) % 4) * 2 + self.y_lo, half, 48, OUTER)
            yield ref, ref, along(0, step)
        elif hop == 3:
            for other in (1, 2, 3):
                for y_lo, step in ((0, 1), (1, 3)):
                    ref = self.part(((x + other) % 4) * 2 + y_lo, half, 48, INNER)
                    yield ref, ref, along(2, step)
                ref = self.part(((x + other) % 4) * 2 + self.y_lo, half, 48, OUTER)
                yield ref, ref, along(2, 1 + 2 * ((other + me[3]) % 2))
        elif hop == 4:
            for other, step in enumerate((1, 3, 1, 3)):
                ref = self.part(other * 2 + self.y_lo, 0, 96, OUTER)
                yield ref, ref, along(1, step)
            ref = self.part(x * 2 + 1 - self.y_lo, 0, 96, INNER)
            yield ref, ref, (0, 0, 0, 1)
            for other in (1, 2, 3):
                ref = self.part(((x + other) % 4) * 2, 0, 192, INNER)
                yield ref, ref, (0, 0, 0, 1)
        else:
            ref = self.part(x * 2 + 1 - self.y_lo, 0, 96, OUTER)
            yield ref, ref, (0, 0, 0, 1)
            for other in (1, 2, 3):
                ref = self.part(((x + other) % 4) * 2, 0, 192, OUTER)
                yield ref, ref, (0, 0, 0, 1)

    def start(self, hop):
        for src, dst, offset in self.copies(hop):
            pltpu.make_async_remote_copy(
                src_ref=src,
                dst_ref=dst,
                send_sem=self.send_sems.at[hop],
                recv_sem=self.recv_sems.at[hop],
                device_id=neighbour(self.me, offset),
                device_id_type=MESH,
            ).start()

    def _wait(self, sems, hop):
        ref = self.weights.at[:, pl.ds(0, (160, 64, 80, 240, 576, 224)[hop]), pl.ds(0, 384)]
        pltpu.make_async_copy(ref, ref, sems.at[hop]).wait()

    def wait(self, hop):
        self._wait(self.recv_sems, hop)

    def wait_sent(self, hop):
        self._wait(self.send_sems, hop)


def each_octet(body):
    def step(m, carry):
        body(m, m // 8, (m // 2) % 4, m % 2)
        return carry

    lax.fori_loop(0, 16, step, 0)


def mix_kernel(
    tokens,
    gain,
    block_w,
    stride_w,
    proj_w,
    scales,
    normed,
    out_proj,
    out_scale,
    block_v,
    stride_v,
    weights,
    colscale,
    wide,
    rows,
    mixed,
    carried,
    total,
    fwd0,
    fwd1,
    fwd2,
    fwd3,
    ret0,
    ret1,
    ret2,
    ret3,
    load_sems,
    out_sem,
    send_sems,
    recv_sems,
    gather_send,
    gather_recv,
):
    me = coordinates()
    sems = (send_sems, recv_sems)
    loads = [pltpu.make_async_copy(tokens.at[b], normed.at[b], load_sems.at[b]) for b in range(4)]
    loads.append(pltpu.make_async_copy(block_w, block_v, load_sems.at[4]))
    loads.append(pltpu.make_async_copy(stride_w, stride_v, load_sems.at[5]))
    gather = Gather(me, proj_w, weights, gather_send, gather_recv)
    loads.append(pltpu.make_async_copy(proj_w, gather.shard(gather.mine), load_sems.at[6]))
    for load in loads[:4]:
        load.start()
    barrier = pltpu.get_barrier_semaphore()
    for offset in PARTNERS:
        pl.semaphore_signal(barrier, inc=1, device_id=neighbour(me, offset), device_id_type=MESH)

    loads[4].start()

    for b in range(4):
        loads[b].wait()

        def norm(i, carry, b=b):
            r = pl.ds(pl.multiple_of(i * 128, 128), 128)
            tiles = [pl.ds(n * WIDTH, WIDTH) for n in range(CHUNKS)]
            squares = jnp.zeros((128, WIDTH), jnp.float32)
            for c in tiles:
                x = normed[b, r, c].astype(jnp.float32)
                squares = squares + x * x
            scale = lax.rsqrt(jnp.sum(squares, axis=-1, keepdims=True) / 768 + 1e-05)
            for c in tiles:
                x = normed[b, r, c].astype(jnp.float32)
                normed[b, r, c] = (x * scale * gain[c][None, :]).astype(jnp.bfloat16)
            return carry

        lax.fori_loop(0, 4, norm, 0)
    pl.semaphore_wait(barrier, len(PARTNERS))
    gather.start(0)
    loads[4].wait()
    for load in loads[5:]:
        load.start()

    forward = [Journey(me, c, (fwd0, fwd1, fwd2, fwd3), sems, 3 * c) for c in range(CHUNKS)]
    back = [Journey(me, c, (ret0, ret1, ret2, ret3), sems, 3 * (CHUNKS + c)) for c in range(CHUNKS)]

    low = lax.broadcasted_iota(jnp.int32, (8, WIDTH), 0) < 4

    def paired(p, q):
        return jnp.where(low, p, pltpu.roll(q, 4, 0)), jnp.where(low, pltpu.roll(p, 4, 0), q)

    for first, count in ((0, 2), (2, 2), (4, 2)):
        for b in range(4):
            columns = pl.ds(first * WIDTH, count * WIDTH)
            x = jnp.dot(block_v[b], normed[b, :, columns], preferred_element_type=jnp.float32)
            for half in range(count):
                wide[half, pl.ds(b, 512, stride=4), :] = x[:, half * WIDTH : (half + 1) * WIDTH]
        for half in range(count):
            chunk = first + half

            def pack(m, y_hi, z, core, half=half, chunk=chunk):
                for x in range(4):
                    for y_lo in range(2):
                        r = pl.ds(pl.multiple_of((m * 8 + x * 2 + y_lo) * PIECE, PIECE), PIECE)
                        slot = send_slot(ORDERS[chunk], (x, y_hi * 2 + y_lo, z, core))
                        fwd0[(chunk, *slot)] = wide[half, r, :].astype(jnp.bfloat16)

            each_octet(pack)
            forward[chunk].start(0)

    loads[6].wait()
    gather.wait(0)
    gather.start(1)
    for hop in range(2):
        for chunk in range(CHUNKS):
            forward[chunk].wait(hop)
            forward[chunk].start(hop + 1)
        gather.wait(hop + 1)
        gather.start(hop + 2)
    loads[5].wait()

    for chunk in range(CHUNKS):
        forward[chunk].wait(2)

        def split(m, y_hi, z, core, chunk=chunk):
            per_t = [[] for _ in range(4)]
            for x in range(4):
                even, odd = [
                    fwd3[(chunk, *landed_slot(ORDERS[chunk], (x, y_hi * 2 + y_lo, z, core)))].astype(jnp.float32)
                    for y_lo in range(2)
                ]
                for j in range(2):
                    first, second = paired(even[8 * j : 8 * j + 8], odd[8 * j : 8 * j + 8])
                    per_t[2 * j].append(first)
                    per_t[2 * j + 1].append(second)
            r = pl.ds(pl.multiple_of(m * 32, 32), 32)
            for t in range(4):
                rows[t, r, :] = jnp.concatenate(per_t[t], axis=0).astype(jnp.bfloat16)

        each_octet(split)
        for t in range(4):
            mixed[t] = jnp.dot(stride_v[t], rows[t], preferred_element_type=jnp.float32)

        def join(m, y_hi, z, core, chunk=chunk):
            for x in range(4):
                r = pl.ds(pl.multiple_of(m * 32 + x * 8, 8), 8)
                top = paired(mixed[0, r, :], mixed[1, r, :])
                bottom = paired(mixed[2, r, :], mixed[3, r, :])
                for y_lo in range(2):
                    slot = send_slot(ORDERS[chunk], (x, y_hi * 2 + y_lo, z, core))
                    ret0[(chunk, *slot)] = jnp.concatenate([top[y_lo], bottom[y_lo]], axis=0).astype(jnp.bfloat16)

        each_octet(join)
        back[chunk].start(0)

    gather.wait(3)
    gather.start(4)
    for chunk in range(CHUNKS):
        back[chunk].wait(0)
        back[chunk].start(1)
    gather.wait(4)
    gather.start(5)

    def scale_columns(k):
        def add_squares(i, sums):
            w = weights[k, pl.ds(pl.multiple_of(i * 64, 64), 64), :].astype(jnp.float32)
            return sums + jnp.sum((w * w).reshape(8, 8, 768), axis=0)

        sums = lax.fori_loop(0, 12, add_squares, jnp.zeros((8, 768), jnp.float32))
        squares = jnp.sum(sums, axis=0, keepdims=True)
        colscale[pl.ds(k, 1), :] = scales[pl.ds(k, 1), :] * lax.rsqrt(squares + 1e-06)

    scale_columns(0)
    scale_columns(1)

    def gate_block(i):
        r = pl.ds((i % 2) * 256, 256)
        gate = jnp.dot(normed[i // 2, r, :], weights[1], preferred_element_type=jnp.float32)
        gate = (gate * colscale[pl.ds(1, 1), :]).astype(jnp.bfloat16).astype(jnp.float32)
        gate = gate / (1.0 + jnp.exp(-gate)) * colscale[pl.ds(0, 1), :]
        normed[i // 2, r, :] = gate.astype(jnp.bfloat16)

    for i in range(8):
        gate_block(i)
    for chunk in range(CHUNKS):
        back[chunk].wait(1)
        back[chunk].start(2)
    gather.wait(5)
    scale_columns(2)
    out_scale[...] = colscale[pl.ds(2, 1), :]
    store = pltpu.make_async_copy(weights.at[2], out_proj, out_sem)
    store.start()

    for chunk in range(CHUNKS):
        back[chunk].wait(2)

        def unpack(m, y_hi, z, core, chunk=chunk):
            for x in range(4):
                for y_lo in range(2):
                    r = pl.ds(pl.multiple_of((m * 8 + x * 2 + y_lo) * PIECE, PIECE), PIECE)
                    slot = landed_slot(ORDERS[chunk], (x, y_hi * 2 + y_lo, z, core))
                    wide[chunk % 2, r, :] = ret3[(chunk, *slot)].astype(jnp.float32)

        each_octet(unpack)
        group = [g for g in GROUPS if chunk in g][0]
        place = pl.ds((chunk - group[0]) * WIDTH, WIDTH)
        for a in range(4):
            carried[a, :, place] = wide[chunk % 2, pl.ds(a, 512, stride=4), :].astype(jnp.bfloat16)
        if chunk != group[-1]:
            continue
        left, right = pl.ds(0, len(group) * WIDTH), pl.ds(group[0] * WIDTH, len(group) * WIDTH)
        for a in range(4):
            part = jnp.dot(carried[a, :, left], weights[0, right, :], preferred_element_type=jnp.float32)
            if group != GROUPS[0]:
                part = total[a] + part
            if group == GROUPS[-1]:
                normed[a] = (part * normed[a].astype(jnp.float32)).astype(jnp.bfloat16)
            else:
                total[a] = part
    for chunk in range(CHUNKS):
        for hop in range(3):
            forward[chunk].wait_sent(hop, rows)
            back[chunk].wait_sent(hop, rows)
    for hop in range(6):
        gather.wait_sent(hop)
    store.wait()


def mix(tokens, gain, block_w, stride_w, proj_w, scales):
    sent = (CHUNKS, 4, 2, 4, 4, PIECE, WIDTH)
    half_way = (CHUNKS, 4, 4, 2, 4, PIECE, WIDTH)
    landed = (CHUNKS, 4, 4, 4, 2, PIECE, WIDTH)
    bf16, f32 = jnp.bfloat16, jnp.float32
    hbm, vmem = pl.BlockSpec(memory_space=pl.ANY), pl.BlockSpec(memory_space=pltpu.VMEM)
    return pl.pallas_call(
        mix_kernel,
        out_shape=[
            pltpu.VMEM((4, 512, 768), bf16),
            pltpu.VMEM((768, 768), bf16),
            pltpu.VMEM((1, 768), f32),
        ],
        in_specs=[hbm, vmem, hbm, hbm, hbm, vmem],
        out_specs=[vmem, hbm, vmem],
        scratch_shapes=[
            pltpu.VMEM((4, 512, 512), bf16),
            pltpu.VMEM((4, 512, 512), bf16),
            pltpu.VMEM((3, 768, 768), bf16),
            pltpu.VMEM((3, 768), f32),
            pltpu.VMEM((2, 2048, WIDTH), f32),
            pltpu.VMEM((4, 512, WIDTH), bf16),
            pltpu.VMEM((4, 512, WIDTH), f32),
            pltpu.VMEM((4, 512, 3 * WIDTH), bf16),
            pltpu.VMEM((4, 512, 768), f32),
            *[pltpu.VMEM(s, bf16) for s in (sent, sent, half_way, landed)],
            *[pltpu.VMEM(s, bf16) for s in (sent, sent, half_way, landed)],
            pltpu.SemaphoreType.DMA((7,)),
            pltpu.SemaphoreType.DMA,
            *[pltpu.SemaphoreType.DMA((6 * CHUNKS,)) for _ in range(2)],
            *[pltpu.SemaphoreType.DMA((6,)) for _ in range(2)],
        ],
        compiler_params=pltpu.CompilerParams(collective_id=0, has_side_effects=True, vmem_limit_bytes=52 << 20),
        name="monarch_mix",
    )(tokens, gain, block_w, stride_w, proj_w, scales)


def project_kernel(hidden, weight, scale, out, result, sems):
    stores = []
    for i in range(8):
        r = pl.ds(i % 2 * 256, 256)
        product = jnp.dot(hidden[i // 2, r, :], weight[...], preferred_element_type=jnp.float32)
        result[i // 2, r, :] = (product * scale[...]).astype(jnp.bfloat16)
        stores.append(pltpu.make_async_copy(result.at[i // 2, r], out.at[i // 2, r], sems.at[i]))
        stores[-1].start()
    for store in stores:
        store.wait()


def project_out(hidden, weight, scale):
    vmem = pl.BlockSpec(memory_space=pltpu.VMEM)
    return pl.pallas_call(
        project_kernel,
        out_shape=jax.ShapeDtypeStruct(hidden.shape, jnp.bfloat16),
        in_specs=[vmem, vmem, vmem],
        out_specs=pl.BlockSpec(memory_space=pl.ANY),
        scratch_shapes=[pltpu.VMEM(hidden.shape, jnp.bfloat16), pltpu.SemaphoreType.DMA((8,))],
        compiler_params=pltpu.CompilerParams(vmem_limit_bytes=24 << 20),
        name="project_out",
    )(
        pltpu.with_memory_space_constraint(hidden, pltpu.VMEM),
        pltpu.with_memory_space_constraint(weight, pltpu.VMEM),
        pltpu.with_memory_space_constraint(scale, pltpu.VMEM),
    )


def local(tokens, norm_gain, block_weights, stride_weights, proj_weights, proj_scales):
    channels = tokens.shape[-1]
    hidden, out_weight, out_scale = mix(
        tokens.reshape(4, 512, channels), norm_gain, block_weights, stride_weights, proj_weights, proj_scales
    )
    return project_out(hidden, out_weight, out_scale).reshape(tokens.shape)


def solution(mesh):
    placed = (
        P(None, ("ctx", "chan"), None),
        P(),
        P(("ctx", "chan"), None, None),
        P(("ctx", "chan"), None, None),
        P(None, "chan", None),
        P(),
    )
    return jax.shard_map(
        local, mesh=mesh, in_specs=placed, out_specs=P(None, ("ctx", "chan"), None), check_vma=False
    )
```
